32 devices in a mesh: layer: 2 (over y), blk: 4 (over z), tok: 2 (over x), rep: 2 (over core).
Axes of the slice: x: 2, y: 2, z: 4, core: 2. Of those that a mesh axis runs over, the one named last changes fastest.
Arguments:
- tokens: bfloat16 [1024, 8192], P(('layer', 'tok', 'rep'), 'blk'), parts along dimension 0, may hold values from -6 to 6
- teacher: bfloat16 [16384, 14336], P(('layer', 'blk'), ('tok', 'rep')), parts along dimension 0, may hold values from -0.0625 to 0.0625
- left_blocks: bfloat16 [128, 8192], P(('layer', 'blk')), parts along dimension 0, may hold values from -0.5 to 0.5
- right_blocks: bfloat16 [128, 14336], P(('layer', 'blk')), parts along dimension 0, may hold values from -0.75 to 0.75
Outputs:
- grad_left: float32 [128, 8192], P(('layer', 'blk'), ('tok', 'rep')), parts along dimension 0
- grad_right: float32 [128, 14336], P(('layer', 'blk'), ('tok', 'rep')), parts along dimension 0
The draws below stay inside these ranges and needn't reach their ends.
There are 2 independent parts, one for each index of `layer`. The reference program is written for one: setup_inputs(seed, part) draws one part's arguments, and reference() takes and returns one part's arrays. A program takes and returns all parts, laid end to end along the dimension named above; each array names one. Nothing has to cross between parts.
All inputs are finite; a program needn't handle non-finite values.
Results may differ from the reference program's by a relative error of at most 0.009.
Values may be sent and summed in bfloat16 or wider, within the bound.
No kernel may reach another device: no remote copies, remote signals or barrier semaphores. Data moves between devices by JAX's collectives and lax.ppermute only.
A program may use at most 64 MiB of HBM per device.

```python
import jax
import jax.numpy as jnp
from jax import lax

D = 8192
F = 14336
NB = 64
TOKENS = 512
BI = 128
FB = 224
PANEL = 2048
N_BLK = 4


def level_of(own_key, shape, shards, low, top_value):
    level = 1.0
    for axis_at, blocks in shards:
        draws = jax.random.uniform(jax.random.fold_in(jax.random.fold_in(own_key, 6), axis_at), (blocks,), jnp.float32, low / len(shards), top_value / len(shards))
        level = level * jnp.repeat(jnp.exp(draws), shape[axis_at] // blocks).reshape((-1,) + (1,) * (len(shape) - 1 - axis_at))
    return level


def gaussian(rng, shape, width, limit, cuts=(), held_as=jnp.bfloat16):
    entries = width * jax.random.normal(rng, shape, jnp.float32)
    if cuts:
        entries = entries * level_of(rng, shape, cuts, -0.22, 0.18)
    return jnp.clip(entries, -limit, limit).astype(held_as)


def setup_inputs(seed: int = 0, part: int = 0) -> dict:
    splits = jax.random.split(jax.random.key(seed), 5)
    part_keys = jax.random.split(jax.random.fold_in(splits[4], part), 5)
    return {
        "tokens": gaussian(part_keys[0], (TOKENS, D), 1.0, 6.0, ((0, 4), (1, 4))),
        "teacher": gaussian(part_keys[1], (D, F), D ** -0.5, 0.0625, ((0, 4), (1, 4))),
        "left_blocks": gaussian(part_keys[2], (NB, BI * NB), BI ** -0.5, 0.5, ((0, 4),)),
        "right_blocks": gaussian(part_keys[3], (NB, NB * FB), NB ** -0.5, 0.75, ((0, 4),)),
    }


def teacher_output(tokens, teacher):
    def add_panel(index, total):
        rows = lax.dynamic_slice_in_dim(tokens, index * PANEL, PANEL, 1)
        weights = lax.dynamic_slice_in_dim(teacher, index * PANEL, PANEL, 0)
        rounded = jnp.dot(rows, weights, preferred_element_type=jnp.float32).astype(jnp.bfloat16)
        rounded = lax.optimization_barrier(rounded)
        return total + rounded.astype(jnp.float32)

    start = jnp.zeros((TOKENS, F), jnp.float32)
    return lax.fori_loop(0, N_BLK, add_panel, start)


def reference(tokens, teacher, left_blocks, right_blocks):
    x_blocks = tokens.reshape(TOKENS, NB, BI).astype(jnp.float32)
    left = left_blocks.reshape(NB, BI, NB).astype(jnp.float32)
    right = right_blocks.reshape(NB, NB, FB).astype(jnp.float32)
    hidden = jnp.einsum("tbj,bjk->tbk", x_blocks, left).astype(jnp.bfloat16)
    hidden_wide = hidden.astype(jnp.float32)
    student = jnp.einsum("tbk,kbo->tko", hidden_wide, right).reshape(TOKENS, F)
    target = teacher_output(tokens, teacher)
    scale = float(TOKENS) ** -0.5
    grad_out = ((student - target) * scale).astype(jnp.bfloat16)
    grad_wide = grad_out.reshape(TOKENS, NB, FB).astype(jnp.float32)
    grad_right = jnp.einsum("tbk,tko->kbo", hidden_wide, grad_wide).reshape(NB, NB * FB)
    back = jnp.einsum("tko,kbo->tbk", grad_wide, right).astype(jnp.bfloat16)
    grad_left = jnp.einsum("tbj,tbk->bjk", x_blocks, back.astype(jnp.float32)).reshape(NB, BI * NB)
    return grad_left, grad_right
```

```python
import functools

import jax
import jax.numpy as jnp
from jax import lax
from jax.experimental import pallas as pl
from jax.experimental.pallas import tpu as pltpu
from jax.sharding import PartitionSpec as P

D = 8192
F = 14336
NB = 64
BI = D // NB
FB = F // NB
GROUP = 4
COLS = GROUP * FB
BF = jnp.bfloat16
F32 = jnp.float32
NT = (((1,), (1,)), ((), ()))
TN = (((0,), (0,)), ((), ()))


def residual_kernel(scale, z_ref, tok_ref, teacher_ref, hid_ref, own_ref, right_ref, resid_ref, back_ref):
    target = jnp.dot(tok_ref[...], teacher_ref[...], preferred_element_type=F32)
    student = lax.dot_general(hid_ref[...], own_ref[0, 0], TN, preferred_element_type=F32)
    resid = ((student - target) * scale).astype(BF)
    resid_ref[...] = resid
    n_z, rows, _ = right_ref.shape[1:]
    right = right_ref[0].reshape(n_z * rows, COLS)
    back = lax.dot_general(right, resid, NT, preferred_element_type=F32)
    back_ref[...] = back.astype(BF).reshape(back_ref.shape)


def residual(z, tokens, teacher, hidden, right, scale):
    t, depth = tokens.shape
    n_q, n_z, rows, _ = right.shape
    cols = teacher.shape[1]
    return pl.pallas_call(
        functools.partial(residual_kernel, scale),
        grid_spec=pltpu.PrefetchScalarGridSpec(
            num_scalar_prefetch=1,
            grid=(n_q,),
            in_specs=[
                pl.BlockSpec((t, depth), lambda q, z: (0, 0)),
                pl.BlockSpec((depth, COLS), lambda q, z: (0, q)),
                pl.BlockSpec((rows, t), lambda q, z: (q, 0)),
                pl.BlockSpec((1, 1, rows, COLS), lambda q, z: (q, z[0], 0, 0)),
                pl.BlockSpec((1, n_z, rows, COLS), lambda q, z: (q, 0, 0, 0)),
            ],
            out_specs=[
                pl.BlockSpec((t, COLS), lambda q, z: (0, q)),
                pl.BlockSpec((n_z, rows, t), lambda q, z: (0, q, 0)),
            ],
        ),
        out_shape=[
            jax.ShapeDtypeStruct((t, cols), BF),
            jax.ShapeDtypeStruct((n_z, n_q * rows, t), BF),
        ],
        compiler_params=pltpu.CompilerParams(vmem_limit_bytes=40 * 1024 * 1024),
        cost_estimate=pl.CostEstimate(
            flops=2 * t * cols * (depth + 256), bytes_accessed=2 * depth * cols, transcendentals=0
        ),
        name="residual",
    )(z, tokens, teacher, hidden, right, right)


def grad_right_kernel(hid_ref, resid_ref, out_ref):
    n_z, rows, t = hid_ref.shape
    per_z = rows // GROUP
    prod = jnp.dot(hid_ref[...].reshape(n_z * rows, t), resid_ref[...], preferred_element_type=F32)
    prod = prod.reshape(n_z, GROUP, per_z, COLS)
    block = lax.broadcasted_iota(jnp.int32, (n_z, per_z, COLS), 2) // FB
    total = prod[:, 0]
    for k in range(1, GROUP):
        total = jnp.where(block == k, prod[:, k], total)
    out_ref[...] = total.astype(BF)


def grad_right_partial(hidden, resid):
    n_z, rows, t = hidden.shape
    cols = resid.shape[1]
    n_q = cols // COLS
    per_z = rows // (n_q * GROUP)
    return pl.pallas_call(
        grad_right_kernel,
        grid=(n_q,),
        in_specs=[
            pl.BlockSpec((n_z, rows // n_q, t), lambda q: (0, q, 0)),
            pl.BlockSpec((t, COLS), lambda q: (0, q)),
        ],
        out_specs=pl.BlockSpec((n_z, per_z, COLS), lambda q: (0, 0, q)),
        out_shape=jax.ShapeDtypeStruct((n_z, per_z, cols), BF),
        compiler_params=pltpu.CompilerParams(vmem_limit_bytes=40 * 1024 * 1024),
        cost_estimate=pl.CostEstimate(
            flops=2 * t * cols * 256, bytes_accessed=2 * t * cols, transcendentals=0
        ),
        name="grad_right",
    )(hidden, resid)


def per_device(tokens, teacher, left_blocks, right_blocks):
    n_z = lax.axis_size("blk")
    n_tok = lax.axis_size("tok")
    n_rep = lax.axis_size("rep")
    n_c = n_tok * n_rep
    z = lax.axis_index("blk")
    c = lax.axis_index(("tok", "rep"))
    tok_dev, depth = tokens.shape
    n_b = left_blocks.shape[0]
    n_k = teacher.shape[1] // FB
    n_q = n_k // GROUP
    scale = float(tok_dev * n_c) ** (-0.5)
    plane = ("blk", "tok", "rep")

    def swap(x, axis, s):
        n = lax.axis_size(axis)
        return lax.ppermute(x, axis, [(i, i ^ s) for i in range(n)])

    right_here = lax.ppermute(
        right_blocks, plane, [(a * n_c + b, b * n_c + a) for a in range(n_z) for b in range(n_c)]
    )

    chips = []
    for s in range(n_tok):
        own = tokens if s == 0 else swap(tokens, "tok", s)
        if n_rep == 1:
            chips.append(own)
        else:
            chips.append(jnp.concatenate([own] + [swap(own, "rep", r) for r in range(1, n_rep)], axis=0))

    left = left_blocks.reshape(n_b * BI, NB)
    rows_kb = n_k * n_b
    pick = (
        lax.broadcasted_iota(jnp.int32, (rows_kb, NB), 0) // n_b + c * n_k
        == lax.broadcasted_iota(jnp.int32, (rows_kb, NB), 1)
    ).astype(BF)
    diag = (
        lax.broadcasted_iota(jnp.int32, (rows_kb, n_b * BI), 0) % n_b
        == lax.broadcasted_iota(jnp.int32, (rows_kb, n_b * BI), 1) // BI
    )
    spread = lax.dot_general(pick, left, NT, preferred_element_type=F32)
    spread = jnp.where(diag, spread, 0.0).astype(BF)

    r = right_here.reshape(n_q, GROUP, n_z, n_b, FB).transpose(0, 2, 1, 3, 4)
    eye = jnp.eye(GROUP, dtype=BF)
    right_diag = (r[:, :, :, :, None, :] * eye[None, None, :, None, :, None]).reshape(
        n_q, n_z, GROUP * n_b, COLS
    )

    z_scalar = jnp.reshape(z, (1,)).astype(jnp.int32)
    hid_all, resids, backs = [], [], []
    for x in chips:
        hid = lax.dot_general(spread, x, NT, preferred_element_type=F32).astype(BF)
        hid_all.append([hid] + [swap(hid, "blk", s) for s in range(1, n_z)])
        resid, back = residual(z_scalar, x, teacher, hid, right_diag, scale)
        resids.append(resid)
        total = None
        for s in range(n_z):
            piece = lax.dynamic_index_in_dim(back, z ^ s, 0, keepdims=False)
            if s:
                piece = swap(piece, "blk", s)
            piece = piece.astype(F32)
            total = piece if total is None else total + piece
        backs.append(total.astype(BF))

    x_all = jnp.concatenate(chips, axis=0)
    back_all = jnp.concatenate(backs, axis=1)
    prod = jnp.dot(back_all, x_all, preferred_element_type=F32)
    gl = jnp.where(diag, prod, 0.0).reshape(n_k, n_b, n_b * BI).sum(1).astype(BF)
    gl = gl.reshape(n_k, n_b, n_c, BI // n_c).transpose(2, 1, 3, 0)
    got = []
    for s in range(n_c):
        piece = lax.dynamic_index_in_dim(gl, c ^ s, 0, keepdims=False)
        if s:
            piece = lax.ppermute(piece, ("tok", "rep"), [(i, i ^ s) for i in range(n_c)])
        got.append(piece)
    got = jnp.stack(got, 0)
    order = jnp.arange(n_c) ^ c
    grad_left = jnp.take(got, order, axis=0).transpose(1, 2, 0, 3).reshape(n_b, -1).astype(F32)

    hid_cat = jnp.stack(
        [jnp.concatenate([h[s] for h in hid_all], axis=1) for s in range(n_z)], axis=0
    )
    gr = grad_right_partial(hid_cat, jnp.concatenate(resids, axis=0))
    total = None
    for s in range(n_z):
        perm = [(a * n_c + b, b * n_c + (a ^ s)) for a in range(n_z) for b in range(n_c)]
        piece = lax.ppermute(gr[s], plane, perm).astype(F32)
        total = piece if total is None else total + piece
    grad_right = total.reshape(n_b, n_k, FB).transpose(1, 0, 2).reshape(n_k, n_b * FB)
    return grad_left, grad_right


def solution(mesh):
    return jax.shard_map(
        per_device,
        mesh=mesh,
        in_specs=(
            P(("layer", "tok", "rep"), "blk"),
            P(("layer", "blk"), ("tok", "rep")),
            P(("layer", "blk"), None),
            P(("layer", "blk"), None),
        ),
        out_specs=(P(("layer", "blk"), ("tok", "rep")), P(("layer", "blk"), ("tok", "rep"))),
        check_vma=False,
    )
```

```python
import functools

import jax
import jax.numpy as jnp
from jax import lax
from jax.experimental import pallas as pl
from jax.experimental.pallas import tpu as pltpu
from jax.sharding import PartitionSpec as P

D = 8192
F = 14336
NB = 64
BI = D // NB
FB = F // NB
GROUP = 4
COLS = GROUP * FB
BF = jnp.bfloat16
F32 = jnp.float32
NT = (((1,), (1,)), ((), ()))
TN = (((0,), (0,)), ((), ()))
VMEM = 40 * 1024 * 1024


def cost(flops, nbytes):
    return pl.CostEstimate(flops=flops, bytes_accessed=nbytes, transcendentals=0)


def rows_of(refs):
    return jnp.concatenate([r[...] for r in refs], axis=0) if len(refs) > 1 else refs[0][...]


def target_kernel(*refs):
    *tok_refs, teacher_ref, out_ref = refs
    out_ref[...] = jnp.dot(rows_of(tok_refs), teacher_ref[...], preferred_element_type=F32).astype(BF)


def target(tokens, teacher):
    t, depth = tokens[0].shape
    cols = teacher.shape[1]
    block = 512 if cols % 512 == 0 else COLS
    total = t * len(tokens)
    return pl.pallas_call(
        target_kernel,
        grid=(cols // block,),
        in_specs=[pl.BlockSpec((t, depth), lambda q: (0, 0))] * len(tokens)
        + [pl.BlockSpec((depth, block), lambda q: (0, q))],
        out_specs=pl.BlockSpec((total, block), lambda q: (0, q)),
        out_shape=jax.ShapeDtypeStruct((total, cols), BF),
        compiler_params=pltpu.CompilerParams(vmem_limit_bytes=VMEM),
        cost_estimate=cost(2 * total * cols * depth, 2 * depth * cols),
        name="target",
    )(*tokens, teacher)


def spread_kernel(in_ref, out_ref):
    n_z, rows, _ = in_ref.shape
    tile = (
        lax.broadcasted_iota(jnp.int32, (FB, COLS), 0)
        == lax.broadcasted_iota(jnp.int32, (FB, COLS), 1) % FB
    )
    wide = jnp.dot(
        in_ref[...].reshape(n_z * rows, FB), tile.astype(F32).astype(BF), preferred_element_type=F32
    ).reshape(n_z, rows, COLS)
    shape = (n_z, rows, COLS)
    own = lax.broadcasted_iota(jnp.int32, shape, 1) // (rows // GROUP) == lax.broadcasted_iota(
        jnp.int32, shape, 2
    ) // FB
    out_ref[0] = jnp.where(own, wide, 0.0).astype(BF)


def spread_right(right, n_q):
    n_z, rows, _ = right.shape
    return pl.pallas_call(
        spread_kernel,
        grid=(n_q,),
        in_specs=[pl.BlockSpec((n_z, rows // n_q, FB), lambda q: (0, q, 0))],
        out_specs=pl.BlockSpec((1, n_z, rows // n_q, COLS), lambda q: (q, 0, 0, 0)),
        out_shape=jax.ShapeDtypeStruct((n_q, n_z, rows // n_q, COLS), BF),
        compiler_params=pltpu.CompilerParams(vmem_limit_bytes=VMEM),
        cost_estimate=cost(2 * n_z * rows * FB * COLS, 4 * n_z * rows * COLS),
        name="spread_right",
    )(right)


def project_kernel(scale, part_ref, hid_ref, right_ref, resid_ref, back_ref):
    n_z, rows, _ = right_ref.shape[1:]
    student = lax.dot_general(hid_ref[...], right_ref[0, 0], TN, preferred_element_type=F32)
    resid = ((student - part_ref[...].astype(F32)) * scale).astype(BF)
    resid_ref[...] = resid
    right = right_ref[0].reshape(n_z * rows, COLS)
    back = lax.dot_general(right, resid, NT, preferred_element_type=F32)
    back_ref[...] = back.astype(BF).reshape(back_ref.shape)


def project(part, hidden, right, scale):
    t, cols = part.shape
    n_q, n_z, rows, _ = right.shape
    return pl.pallas_call(
        functools.partial(project_kernel, scale),
        grid=(n_q,),
        in_specs=[
            pl.BlockSpec((t, COLS), lambda q: (0, q)),
            pl.BlockSpec((rows, t), lambda q: (q, 0)),
            pl.BlockSpec((1, n_z, rows, COLS), lambda q: (q, 0, 0, 0)),
        ],
        out_specs=[
            pl.BlockSpec((t, COLS), lambda q: (0, q)),
            pl.BlockSpec((n_z, rows, t), lambda q: (0, q, 0)),
        ],
        out_shape=[
            jax.ShapeDtypeStruct((t, cols), BF),
            jax.ShapeDtypeStruct((n_z, n_q * rows, t), BF),
        ],
        compiler_params=pltpu.CompilerParams(vmem_limit_bytes=VMEM),
        cost_estimate=cost(2 * t * cols * n_z * rows * 2, 6 * t * cols),
        name="project",
    )(part, hidden, right)


def grad_right_kernel(n_z, halves, *refs):
    hid_refs, resid_refs, out_ref = refs[: n_z * halves], refs[n_z * halves : -1], refs[-1]
    rows = hid_refs[0].shape[0]
    per_z = rows // GROUP
    prod = None
    for h in range(halves):
        hid = rows_of(hid_refs[h * n_z : (h + 1) * n_z])
        term = jnp.dot(hid, resid_refs[h][...], preferred_element_type=F32)
        prod = term if prod is None else prod + term
    prod = prod.reshape(n_z, GROUP, per_z, COLS)
    block = lax.broadcasted_iota(jnp.int32, (n_z, per_z, COLS), 2) // FB
    total = prod[:, 0]
    for k in range(1, GROUP):
        total = jnp.where(block == k, prod[:, k], total)
    out_ref[...] = total.astype(BF)


def grad_right_partial(hidden, resids):
    halves, n_z = len(hidden), len(hidden[0])
    rows, t = hidden[0][0].shape
    cols = resids[0].shape[1]
    n_q = cols // COLS
    per_z = rows // (n_q * GROUP)
    return pl.pallas_call(
        functools.partial(grad_right_kernel, n_z, halves),
        grid=(n_q,),
        in_specs=[pl.BlockSpec((rows // n_q, t), lambda q: (q, 0))] * (halves * n_z)
        + [pl.BlockSpec((t, COLS), lambda q: (0, q))] * halves,
        out_specs=pl.BlockSpec((n_z, per_z, COLS), lambda q: (0, 0, q)),
        out_shape=jax.ShapeDtypeStruct((n_z, per_z, cols), BF),
        compiler_params=pltpu.CompilerParams(vmem_limit_bytes=VMEM),
        cost_estimate=cost(2 * halves * t * cols * n_z * rows // n_q, 2 * halves * t * cols),
        name="grad_right",
    )(*[h for hs in hidden for h in hs], *resids)


def grad_left_kernel(n_z, halves, n_k, *refs):
    per = halves * n_z
    back_refs, tok_refs, out_ref = refs[:per], refs[per:-1], refs[-1]
    pieces = len(tok_refs) // halves
    prod = None
    for h in range(halves):
        total = back_refs[h * n_z][0].astype(F32)
        for s in range(1, n_z):
            total = total + back_refs[h * n_z + s][...].astype(F32)
        term = jnp.dot(
            total.astype(BF),
            rows_of(tok_refs[h * pieces : (h + 1) * pieces]),
            preferred_element_type=F32,
        )
        prod = term if prod is None else prod + term
    rows, block = prod.shape
    n_b = rows // n_k
    prod = prod.reshape(n_k, n_b, block)
    at = pl.program_id(0) * (block // BI)
    own = lax.broadcasted_iota(jnp.int32, prod.shape, 1) == at + lax.broadcasted_iota(
        jnp.int32, prod.shape, 2
    ) // BI
    out_ref[...] = jnp.where(own, prod, 0.0).sum(1).astype(BF)


def grad_left_of(backs, tokens, n_k):
    halves, n_z = len(backs), len(backs[0])
    rows, t = backs[0][1].shape
    piece, depth = tokens[0][0].shape
    block = min(depth, 1024)
    first = pl.BlockSpec((1, rows, t), lambda q: (0, 0, 0))
    rest = pl.BlockSpec((rows, t), lambda q: (0, 0))
    flat = [x for h in tokens for x in h]
    return pl.pallas_call(
        functools.partial(grad_left_kernel, n_z, halves, n_k),
        grid=(depth // block,),
        in_specs=([first] + [rest] * (n_z - 1)) * halves
        + [pl.BlockSpec((piece, block), lambda q: (0, q))] * len(flat),
        out_specs=pl.BlockSpec((n_k, block), lambda q: (0, q)),
        out_shape=jax.ShapeDtypeStruct((n_k, depth), BF),
        compiler_params=pltpu.CompilerParams(vmem_limit_bytes=VMEM),
        cost_estimate=cost(2 * halves * t * rows * depth, 2 * halves * t * depth),
        name="grad_left",
    )(*[b for h in backs for b in h], *flat)


def place_kernel(n_b, c_ref, *refs):
    in_refs, out_ref = refs[:-1], refs[-1]
    n_c, n_k = len(in_refs), in_refs[0].shape[0]
    x = rows_of(in_refs)
    row = lax.broadcasted_iota(jnp.int32, (NB, NB), 0)
    col = lax.broadcasted_iota(jnp.int32, (NB, NB), 1)
    pick = row == ((col // n_k) ^ c_ref[0]) * n_k + col % n_k
    got = lax.dot_general(
        x, pick.astype(F32).astype(BF), (((0,), (1,)), ((), ())), preferred_element_type=F32
    )
    for j in range(got.shape[0] // n_b):
        out_ref[:, j * NB : (j + 1) * NB] = got[j * n_b : (j + 1) * n_b]


def place(c, pieces, n_b):
    n = pieces[0].shape[1] // n_b
    return pl.pallas_call(
        functools.partial(place_kernel, n_b),
        in_specs=[pl.BlockSpec(memory_space=pltpu.SMEM)]
        + [pl.BlockSpec(memory_space=pltpu.VMEM)] * len(pieces),
        out_specs=pl.BlockSpec(memory_space=pltpu.VMEM),
        out_shape=jax.ShapeDtypeStruct((n_b, n * NB), F32),
        name="place",
    )(c, *pieces)


def swap(x, axes, s):
    n = lax.axis_size(axes)
    return lax.ppermute(x, axes, [(i, i ^ s) for i in range(n)])


def gather(x, axes):
    got = [x]
    for s in range(1, lax.axis_size(axes)):
        got.append(swap(got[s & (s - 1)], axes, s & -s))
    return got


def pick(x, at):
    return lax.dynamic_index_in_dim(x, at, 0, keepdims=False)


def per_device(tokens, teacher, left_blocks, right_blocks):
    n_z = lax.axis_size("blk")
    n_c = lax.axis_size(("tok", "rep"))
    n_rep = lax.axis_size("rep")
    z = lax.axis_index("blk")
    c = lax.axis_index(("tok", "rep"))
    plane = ("tok", "rep")
    n_b = left_blocks.shape[0]
    n_k = teacher.shape[1] // FB
    n_q = n_k // GROUP
    scale = float(tokens.shape[0] * n_c) ** (-0.5)

    chips = [[own] + [swap(own, "rep", r) for r in range(1, n_rep)] for own in gather(tokens, "tok")]

    share = n_b * FB
    quarter = lax.dynamic_slice_in_dim(right_blocks, c * share, share, 1)
    quarters = jnp.stack(gather(quarter, "blk"), 0)
    here = []
    for s in range(n_c):
        piece = pick(quarters, z ^ c ^ s)
        here.append(swap(piece, plane, s) if s else piece)
    here = jnp.stack(here, 0)
    right = jnp.stack([pick(here, c ^ z ^ s) for s in range(n_z)], 0)
    right = spread_right(right.reshape(n_z, n_k * n_b, FB), n_q)

    left = left_blocks.reshape(n_b * BI, NB)
    rows_kb = n_k * n_b
    take = (
        lax.broadcasted_iota(jnp.int32, (rows_kb, NB), 0) // n_b + c * n_k
        == lax.broadcasted_iota(jnp.int32, (rows_kb, NB), 1)
    ).astype(BF)
    diag = (
        lax.broadcasted_iota(jnp.int32, (rows_kb, n_b * BI), 0) % n_b
        == lax.broadcasted_iota(jnp.int32, (rows_kb, n_b * BI), 1) // BI
    )
    left = lax.dot_general(take, left, NT, preferred_element_type=F32)
    left = jnp.where(diag, left, 0.0).astype(BF)

    hidden, resids, backs = [], [], []
    for x in chips:
        hid = jnp.concatenate(
            [lax.dot_general(left, p, NT, preferred_element_type=F32).astype(BF) for p in x], axis=1
        )
        hidden.append(gather(hid, "blk"))
        resid, back = project(target(x, teacher), hid, right, scale)
        resids.append(resid)
        backs.append([back] + [swap(back[s], "blk", s) for s in range(1, n_z)])

    gl = grad_left_of(backs, chips, n_k)
    gl = gl.reshape(n_k, n_b, n_c, BI // n_c).transpose(2, 0, 3, 1).reshape(n_c, n_k, -1)
    got = []
    for s in range(n_c):
        piece = pick(gl, c ^ s)
        got.append(swap(piece, plane, s) if s else piece)
    grad_left = place(jnp.reshape(c, (1,)).astype(jnp.int32), got, n_b)

    gr = grad_right_partial(hidden, resids)
    there = []
    for s in range(n_c):
        piece = pick(gr, z ^ c ^ s)
        there.append(swap(piece, plane, s) if s else piece)
    there = jnp.stack(there, 0)
    total = None
    for s in range(n_z):
        piece = pick(there, c ^ z ^ s)
        piece = (swap(piece, "blk", s) if s else piece).astype(F32)
        total = piece if total is None else total + piece
    grad_right = total.reshape(n_b, n_k, FB).transpose(1, 0, 2).reshape(n_k, n_b * FB)
    return grad_left, grad_right


def solution(mesh):
    return jax.shard_map(
        per_device,
        mesh=mesh,
        in_specs=(
            P(("layer", "tok", "rep"), "blk"),
            P(("layer", "blk"), ("tok", "rep")),
            P(("layer", "blk"), None),
            P(("layer", "blk"), None),
        ),
        out_specs=(P(("layer", "blk"), ("tok", "rep")), P(("layer", "blk"), ("tok", "rep"))),
        check_vma=False,
    )
```

```python
import functools

import jax
import jax.numpy as jnp
from jax import lax
from jax.experimental import pallas as pl
from jax.experimental.pallas import tpu as pltpu
from jax.sharding import PartitionSpec as P

D = 8192
F = 14336
NB = 64
BI = D // NB
FB = F // NB
GROUP = 4
COLS = GROUP * FB
BF = jnp.bfloat16
F32 = jnp.float32
NT = (((1,), (1,)), ((), ()))
TN = (((0,), (0,)), ((), ()))
SPLIT = 4
VMEM = 40 * 1024 * 1024


def cost(flops, nbytes):
    return pl.CostEstimate(flops=flops, bytes_accessed=nbytes, transcendentals=0)


def rows_of(refs):
    return jnp.concatenate([r[...] for r in refs], axis=0) if len(refs) > 1 else refs[0][...]


def target_kernel(pieces, *refs):
    tok_refs, teacher_refs, out_ref = refs[:pieces], refs[pieces:-1], refs[-1]
    out_ref[...] = jnp.dot(
        rows_of(tok_refs), rows_of(teacher_refs), preferred_element_type=F32
    ).astype(BF)


def target(tokens, teacher):
    t, depth = tokens[0].shape
    cols = teacher.shape[1]
    block = 512 if cols % 512 == 0 else COLS
    total = t * len(tokens)
    return pl.pallas_call(
        functools.partial(target_kernel, len(tokens)),
        grid=(cols // block,),
        in_specs=[pl.BlockSpec((t, depth), lambda q: (0, 0))] * len(tokens)
        + [pl.BlockSpec((depth // SPLIT, block), lambda q, i=i: (i, q)) for i in range(SPLIT)],
        out_specs=pl.BlockSpec((total, block), lambda q: (0, q)),
        out_shape=jax.ShapeDtypeStruct((total, cols), BF),
        compiler_params=pltpu.CompilerParams(vmem_limit_bytes=VMEM),
        cost_estimate=cost(2 * total * cols * depth, 2 * depth * cols),
        name="target",
    )(*tokens, *[teacher] * SPLIT)


def spread_kernel(in_ref, out_ref):
    n_z, rows, _ = in_ref.shape
    tile = (
        lax.broadcasted_iota(jnp.int32, (FB, COLS), 0)
        == lax.broadcasted_iota(jnp.int32, (FB, COLS), 1) % FB
    )
    wide = jnp.dot(
        in_ref[...].reshape(n_z * rows, FB), tile.astype(F32).astype(BF), preferred_element_type=F32
    ).reshape(n_z, rows, COLS)
    shape = (n_z, rows, COLS)
    own = lax.broadcasted_iota(jnp.int32, shape, 1) // (rows // GROUP) == lax.broadcasted_iota(
        jnp.int32, shape, 2
    ) // FB
    out_ref[0] = jnp.where(own, wide, 0.0).astype(BF)


def spread_right(right, n_q):
    n_z, rows, _ = right.shape
    return pl.pallas_call(
        spread_kernel,
        grid=(n_q,),
        in_specs=[pl.BlockSpec((n_z, rows // n_q, FB), lambda q: (0, q, 0))],
        out_specs=pl.BlockSpec((1, n_z, rows // n_q, COLS), lambda q: (q, 0, 0, 0)),
        out_shape=jax.ShapeDtypeStruct((n_q, n_z, rows // n_q, COLS), BF),
        compiler_params=pltpu.CompilerParams(vmem_limit_bytes=VMEM),
        cost_estimate=cost(2 * n_z * rows * FB * COLS, 4 * n_z * rows * COLS),
        name="spread_right",
    )(right)


def project_kernel(scale, part_ref, hid_ref, right_ref, resid_ref, back_ref):
    n_z, rows, _ = right_ref.shape[1:]
    student = lax.dot_general(hid_ref[...], right_ref[0, 0], TN, preferred_element_type=F32)
    resid = ((student - part_ref[...].astype(F32)) * scale).astype(BF)
    resid_ref[...] = resid
    right = right_ref[0].reshape(n_z * rows, COLS)
    back = lax.dot_general(right, resid, NT, preferred_element_type=F32)
    back_ref[...] = back.astype(BF).reshape(back_ref.shape)


def project(part, hidden, right, scale):
    t, cols = part.shape
    n_q, n_z, rows, _ = right.shape
    return pl.pallas_call(
        functools.partial(project_kernel, scale),
        grid=(n_q,),
        in_specs=[
            pl.BlockSpec((t, COLS), lambda q: (0, q)),
            pl.BlockSpec((rows, t), lambda q: (q, 0)),
            pl.BlockSpec((1, n_z, rows, COLS), lambda q: (q, 0, 0, 0)),
        ],
        out_specs=[
            pl.BlockSpec((t, COLS), lambda q: (0, q)),
            pl.BlockSpec((n_z, rows, t), lambda q: (0, q, 0)),
        ],
        out_shape=[
            jax.ShapeDtypeStruct((t, cols), BF),
            jax.ShapeDtypeStruct((n_z, n_q * rows, t), BF),
        ],
        compiler_params=pltpu.CompilerParams(vmem_limit_bytes=VMEM),
        cost_estimate=cost(2 * t * cols * n_z * rows * 2, 6 * t * cols),
        name="project",
    )(part, hidden, right)


def grad_right_kernel(*refs):
    *hid_refs, resid_ref, out_ref = refs
    n_z, per_z = len(hid_refs), hid_refs[0].shape[0] // GROUP
    prod = jnp.dot(rows_of(hid_refs), resid_ref[...], preferred_element_type=F32)
    prod = prod.reshape(n_z, GROUP, per_z, COLS)
    block = lax.broadcasted_iota(jnp.int32, (n_z, per_z, COLS), 2) // FB
    total = prod[:, 0]
    for k in range(1, GROUP):
        total = jnp.where(block == k, prod[:, k], total)
    out_ref[...] = total.astype(BF)


def grad_right_partial(hidden, resid):
    n_z = len(hidden)
    rows, t = hidden[0].shape
    cols = resid.shape[1]
    n_q = cols // COLS
    per_z = rows // (n_q * GROUP)
    return pl.pallas_call(
        grad_right_kernel,
        grid=(n_q,),
        in_specs=[pl.BlockSpec((rows // n_q, t), lambda q: (q, 0))] * n_z
        + [pl.BlockSpec((t, COLS), lambda q: (0, q))],
        out_specs=pl.BlockSpec((n_z, per_z, COLS), lambda q: (0, 0, q)),
        out_shape=jax.ShapeDtypeStruct((n_z, per_z, cols), BF),
        compiler_params=pltpu.CompilerParams(vmem_limit_bytes=VMEM),
        cost_estimate=cost(2 * t * cols * n_z * rows // n_q, 2 * t * cols),
        name="grad_right",
    )(*hidden, resid)


def grad_left_kernel(n_z, n_k, *refs):
    back_refs, tok_refs, out_ref = refs[:n_z], refs[n_z:-1], refs[-1]
    total = back_refs[0][0].astype(F32)
    for ref in back_refs[1:]:
        total = total + ref[...].astype(F32)
    prod = jnp.dot(total.astype(BF), rows_of(tok_refs), preferred_element_type=F32)
    rows, block = prod.shape
    prod = prod.reshape(n_k, rows // n_k, block)
    at = pl.program_id(0) * (block // BI)
    own = lax.broadcasted_iota(jnp.int32, prod.shape, 1) == at + lax.broadcasted_iota(
        jnp.int32, prod.shape, 2
    ) // BI
    out_ref[...] = jnp.where(own, prod, 0.0).sum(1).astype(BF)


def grad_left_of(backs, tokens, n_k):
    n_z = len(backs)
    rows, t = backs[1].shape
    piece, depth = tokens[0].shape
    block = min(depth, 1024)
    return pl.pallas_call(
        functools.partial(grad_left_kernel, n_z, n_k),
        grid=(depth // block,),
        in_specs=[pl.BlockSpec((1, rows, t), lambda q: (0, 0, 0))]
        + [pl.BlockSpec((rows, t), lambda q: (0, 0))] * (n_z - 1)
        + [pl.BlockSpec((piece, block), lambda q: (0, q))] * len(tokens),
        out_specs=pl.BlockSpec((n_k, block), lambda q: (0, q)),
        out_shape=jax.ShapeDtypeStruct((n_k, depth), BF),
        compiler_params=pltpu.CompilerParams(vmem_limit_bytes=VMEM),
        cost_estimate=cost(2 * t * rows * depth, 2 * t * depth),
        name="grad_left",
    )(*backs, *tokens)


def place_kernel(n_b, c_ref, *refs):
    in_refs, out_ref = refs[:-1], refs[-1]
    n_c, n_k = len(in_refs), in_refs[0].shape[0]
    x = rows_of(in_refs)
    row = lax.broadcasted_iota(jnp.int32, (NB, NB), 0)
    col = lax.broadcasted_iota(jnp.int32, (NB, NB), 1)
    pick = row == ((col // n_k) ^ c_ref[0]) * n_k + col % n_k
    got = lax.dot_general(
        x, pick.astype(F32).astype(BF), (((0,), (1,)), ((), ())), preferred_element_type=F32
    )
    for j in range(got.shape[0] // n_b):
        out_ref[:, j * NB : (j + 1) * NB] = got[j * n_b : (j + 1) * n_b]


def place(c, pieces, n_b):
    n = pieces[0].shape[1] // n_b
    return pl.pallas_call(
        functools.partial(place_kernel, n_b),
        in_specs=[pl.BlockSpec(memory_space=pltpu.SMEM)]
        + [pl.BlockSpec(memory_space=pltpu.VMEM)] * len(pieces),
        out_specs=pl.BlockSpec(memory_space=pltpu.VMEM),
        out_shape=jax.ShapeDtypeStruct((n_b, n * NB), F32),
        name="place",
    )(c, *pieces)


def swap(x, axes, s):
    n = lax.axis_size(axes)
    return lax.ppermute(x, axes, [(i, i ^ s) for i in range(n)])


def gather(x, axes):
    got = [x]
    for s in range(1, lax.axis_size(axes)):
        got.append(swap(got[s & (s - 1)], axes, s & -s))
    return got


def pick(x, at):
    return lax.dynamic_index_in_dim(x, at, 0, keepdims=False)


def per_device(tokens, teacher, left_blocks, right_blocks):
    n_z = lax.axis_size("blk")
    n_c = lax.axis_size(("tok", "rep"))
    z = lax.axis_index("blk")
    c = lax.axis_index(("tok", "rep"))
    plane = ("tok", "rep")
    n_b = left_blocks.shape[0]
    n_k = teacher.shape[1] // FB
    n_q = n_k // GROUP
    scale = float(tokens.shape[0] * n_c) ** (-0.5)

    pieces = [p for own in gather(tokens, "tok") for p in gather(own, "rep")]

    half = n_k // 2
    sides = []
    for i, side in enumerate((0, n_c // 2)):
        perm = [(a * n_c + b, (b ^ side) * n_c + a) for a in range(n_z) for b in range(n_c)]
        sides.append(lax.ppermute(right_blocks[i * half : (i + 1) * half], ("blk",) + plane, perm))
    right = jnp.concatenate(sides, axis=0).reshape(n_k, n_z, n_b * FB)
    right = jnp.stack([lax.dynamic_index_in_dim(right, z ^ s, 1, keepdims=False) for s in range(n_z)], 0)
    right = spread_right(right.reshape(n_z, n_k * n_b, FB), n_q)

    left = left_blocks.reshape(n_b * BI, NB)
    rows_kb = n_k * n_b
    take = (
        lax.broadcasted_iota(jnp.int32, (rows_kb, NB), 0) // n_b + c * n_k
        == lax.broadcasted_iota(jnp.int32, (rows_kb, NB), 1)
    ).astype(BF)
    diag = (
        lax.broadcasted_iota(jnp.int32, (rows_kb, n_b * BI), 0) % n_b
        == lax.broadcasted_iota(jnp.int32, (rows_kb, n_b * BI), 1) // BI
    )
    left = lax.dot_general(take, left, NT, preferred_element_type=F32)
    left = jnp.where(diag, left, 0.0).astype(BF)

    hid = jnp.concatenate(
        [lax.dot_general(left, p, NT, preferred_element_type=F32).astype(BF) for p in pieces], axis=1
    )
    hidden = gather(hid, "blk")
    resid, back = project(target(pieces, teacher), hid, right, scale)
    backs = [back] + [swap(back[s], "blk", s) for s in range(1, n_z)]

    gl = grad_left_of(backs, pieces, n_k)
    gl = gl.reshape(n_k, n_b, n_c, BI // n_c).transpose(2, 0, 3, 1).reshape(n_c, n_k, -1)
    got = []
    for s in range(n_c):
        piece = pick(gl, c ^ s)
        got.append(swap(piece, plane, s) if s else piece)
    grad_left = place(jnp.reshape(c, (1,)).astype(jnp.int32), got, n_b)

    gr = grad_right_partial(hidden, resid)
    there = []
    for s in range(n_c):
        piece = pick(gr, z ^ c ^ s)
        there.append(swap(piece, plane, s) if s else piece)
    there = jnp.stack(there, 0)
    total = None
    for s in range(n_z):
        piece = pick(there, c ^ z ^ s)
        piece = (swap(piece, "blk", s) if s else piece).astype(F32)
        total = piece if total is None else total + piece
    grad_right = total.reshape(n_b, n_k, FB).transpose(1, 0, 2).reshape(n_k, n_b * FB)
    return grad_left, grad_right


def solution(mesh):
    return jax.shard_map(
        per_device,
        mesh=mesh,
        in_specs=(
            P(("layer", "tok", "rep"), "blk"),
            P(("layer", "blk"), ("tok", "rep")),
            P(("layer", "blk"), None),
            P(("layer", "blk"), None),
        ),
        out_specs=(P(("layer", "blk"), ("tok", "rep")), P(("layer", "blk"), ("tok", "rep"))),
        check_vma=False,
    )
```

```python
import functools

import jax
import jax.numpy as jnp
from jax import lax
from jax.experimental import pallas as pl
from jax.experimental.pallas import tpu as pltpu
from jax.sharding import PartitionSpec as P

D = 8192
F = 14336
NB = 64
BI = D // NB
FB = F // NB
GROUP = 4
COLS = GROUP * FB
BF = jnp.bfloat16
F32 = jnp.float32
NT = (((1,), (1,)), ((), ()))
TN = (((0,), (0,)), ((), ()))
SPLIT = 4
VMEM = 40 * 1024 * 1024


def cost(flops, nbytes):
    return pl.CostEstimate(flops=flops, bytes_accessed=nbytes, transcendentals=0)


def rows_of(refs):
    return jnp.concatenate([r[...] for r in refs], axis=0) if len(refs) > 1 else refs[0][...]


def spread(right):
    n_z, n_k, n_b, _ = right.shape
    rows = n_z * n_k * n_b
    tile = (
        lax.broadcasted_iota(jnp.int32, (FB, COLS), 0)
        == lax.broadcasted_iota(jnp.int32, (FB, COLS), 1) % FB
    )
    wide = jnp.dot(right.reshape(rows, FB), tile.astype(F32).astype(BF), preferred_element_type=F32)
    k_row = lax.broadcasted_iota(jnp.int32, (rows, COLS), 0) // n_b % n_k
    k_col = lax.broadcasted_iota(jnp.int32, (rows, COLS), 1) // FB
    return jnp.where(k_row == k_col, wide, 0.0).astype(BF)


def back_kernel(scale, n_tok, n_hid, n_z, z_ref, *refs):
    tok_refs, refs = refs[:n_tok], refs[n_tok:]
    hid_refs, refs = refs[:n_hid], refs[n_hid:]
    teacher_refs, right_refs, (back_ref, own_ref) = refs[:SPLIT], refs[SPLIT:-2], refs[-2:]
    right = jnp.stack(
        [jnp.concatenate([a[0, :, 0], b[0, :, 0]], axis=0) for a, b in zip(right_refs[:n_z], right_refs[n_z:])],
        axis=0,
    )
    right = spread(right)
    rows = right.shape[0] // n_z
    own_ref[0] = right[:rows]
    folded = jnp.concatenate(
        [lax.dot_general(t[...], right, NT, preferred_element_type=F32).astype(BF) for t in teacher_refs],
        axis=0,
    )
    square = lax.dot_general(right[:rows], right, NT, preferred_element_type=F32).astype(BF)
    hid = jnp.concatenate([h[...] for h in hid_refs], axis=1)
    back = lax.dot_general(hid, square, TN, preferred_element_type=F32) - jnp.dot(
        rows_of(tok_refs), folded, preferred_element_type=F32
    )
    back_ref[...] = (back * scale).T.astype(BF).reshape(back_ref.shape)


def back_partial(z, tokens, hidden, teacher, sides, scale):
    piece, depth = tokens[0].shape
    t = piece * len(tokens)
    cols = teacher.shape[1]
    n_q, half, n_z, n_b, _ = sides[0].shape
    rows = GROUP * n_b
    right_specs = [
        pl.BlockSpec((1, half, 1, n_b, FB), lambda q, z, s=s: (q, 0, z[0] ^ s, 0, 0)) for s in range(n_z)
    ]
    return pl.pallas_call(
        functools.partial(back_kernel, scale, len(tokens), len(hidden), n_z),
        grid_spec=pltpu.PrefetchScalarGridSpec(
            num_scalar_prefetch=1,
            grid=(n_q,),
            in_specs=[pl.BlockSpec((piece, depth), lambda q, z: (0, 0))] * len(tokens)
            + [pl.BlockSpec((rows, h.shape[1]), lambda q, z: (q, 0)) for h in hidden]
            + [pl.BlockSpec((depth // SPLIT, COLS), lambda q, z, i=i: (i, q)) for i in range(SPLIT)]
            + right_specs * 2,
            out_specs=[
                pl.BlockSpec((n_z, rows, t), lambda q, z: (0, q, 0)),
                pl.BlockSpec((1, rows, COLS), lambda q, z: (q, 0, 0)),
            ],
        ),
        out_shape=[
            jax.ShapeDtypeStruct((n_z, n_q * rows, t), BF),
            jax.ShapeDtypeStruct((n_q, rows, COLS), BF),
        ],
        compiler_params=pltpu.CompilerParams(vmem_limit_bytes=VMEM),
        cost_estimate=cost(4 * t * depth * n_z * rows * n_q, 2 * depth * cols),
        name="back",
    )(z, *tokens, *hidden, *[teacher] * SPLIT, *[sides[0]] * n_z, *[sides[1]] * n_z)


def grad_right_kernel(scale, n_tok, n_z, parts, *refs):
    tok_refs, teacher_refs, refs = refs[:n_tok], refs[n_tok : n_tok + SPLIT], refs[n_tok + SPLIT :]
    hid_refs, (right_ref, out_ref) = refs[:-2], refs[-2:]
    target = jnp.dot(rows_of(tok_refs), rows_of(teacher_refs), preferred_element_type=F32)
    hid = [
        jnp.concatenate([r[...] for r in hid_refs[s * parts : (s + 1) * parts]], axis=1) for s in range(n_z)
    ]
    student = lax.dot_general(hid[0], right_ref[0], TN, preferred_element_type=F32)
    resid = ((student - target) * scale).astype(BF)
    prod = jnp.dot(jnp.concatenate(hid, axis=0), resid, preferred_element_type=F32)
    per_z = hid[0].shape[0] // GROUP
    prod = prod.reshape(n_z, GROUP, per_z, COLS)
    block = lax.broadcasted_iota(jnp.int32, (n_z, per_z, COLS), 2) // FB
    total = prod[:, 0]
    for k in range(1, GROUP):
        total = jnp.where(block == k, prod[:, k], total)
    out_ref[...] = total.astype(BF)


def grad_right_partial(tokens, teacher, hidden, right, scale):
    piece, depth = tokens[0].shape
    t = piece * len(tokens)
    cols = teacher.shape[1]
    n_z, parts = len(hidden), len(hidden[0])
    n_q, rows, _ = right.shape
    return pl.pallas_call(
        functools.partial(grad_right_kernel, scale, len(tokens), n_z, parts),
        grid=(n_q,),
        in_specs=[pl.BlockSpec((piece, depth), lambda q: (0, 0))] * len(tokens)
        + [pl.BlockSpec((depth // SPLIT, COLS), lambda q, i=i: (i, q)) for i in range(SPLIT)]
        + [pl.BlockSpec((rows, h.shape[1]), lambda q: (q, 0)) for hs in hidden for h in hs]
        + [pl.BlockSpec((1, rows, COLS), lambda q: (q, 0, 0))],
        out_specs=pl.BlockSpec((n_z, rows // GROUP, COLS), lambda q: (0, 0, q)),
        out_shape=jax.ShapeDtypeStruct((n_z, rows // GROUP, cols), BF),
        compiler_params=pltpu.CompilerParams(vmem_limit_bytes=VMEM),
        cost_estimate=cost(2 * t * cols * (depth + n_z * rows), 2 * depth * cols),
        name="grad_right",
    )(*tokens, *[teacher] * SPLIT, *[h for hs in hidden for h in hs], right)


def grad_left_kernel(n_z, n_k, *refs):
    back_refs, tok_refs, out_ref = refs[:n_z], refs[n_z:-1], refs[-1]
    total = back_refs[0][0].astype(F32)
    for ref in back_refs[1:]:
        total = total + ref[...].astype(F32)
    prod = jnp.dot(total.astype(BF), rows_of(tok_refs), preferred_element_type=F32)
    rows, block = prod.shape
    prod = prod.reshape(n_k, rows // n_k, block)
    at = pl.program_id(0) * (block // BI)
    own = lax.broadcasted_iota(jnp.int32, prod.shape, 1) == at + lax.broadcasted_iota(
        jnp.int32, prod.shape, 2
    ) // BI
    out_ref[...] = jnp.where(own, prod, 0.0).sum(1).astype(BF)


def grad_left_of(backs, tokens, n_k):
    n_z = len(backs)
    rows, t = backs[1].shape
    piece, depth = tokens[0].shape
    block = min(depth, 1024)
    return pl.pallas_call(
        functools.partial(grad_left_kernel, n_z, n_k),
        grid=(depth // block,),
        in_specs=[pl.BlockSpec((1, rows, t), lambda q: (0, 0, 0))]
        + [pl.BlockSpec((rows, t), lambda q: (0, 0))] * (n_z - 1)
        + [pl.BlockSpec((piece, block), lambda q: (0, q))] * len(tokens),
        out_specs=pl.BlockSpec((n_k, block), lambda q: (0, q)),
        out_shape=jax.ShapeDtypeStruct((n_k, depth), BF),
        compiler_params=pltpu.CompilerParams(vmem_limit_bytes=VMEM),
        cost_estimate=cost(2 * t * rows * depth, 2 * t * depth),
        name="grad_left",
    )(*backs, *tokens)


def place_kernel(n_b, c_ref, *refs):
    in_refs, out_ref = refs[:-1], refs[-1]
    n_c, n_k = len(in_refs), in_refs[0].shape[0]
    x = rows_of(in_refs)
    row = lax.broadcasted_iota(jnp.int32, (NB, NB), 0)
    col = lax.broadcasted_iota(jnp.int32, (NB, NB), 1)
    pick = row == ((col // n_k) ^ c_ref[0]) * n_k + col % n_k
    got = lax.dot_general(
        x, pick.astype(F32).astype(BF), (((0,), (1,)), ((), ())), preferred_element_type=F32
    )
    for j in range(got.shape[0] // n_b):
        out_ref[:, j * NB : (j + 1) * NB] = got[j * n_b : (j + 1) * n_b]


def place(c, pieces, n_b):
    n = pieces[0].shape[1] // n_b
    return pl.pallas_call(
        functools.partial(place_kernel, n_b),
        in_specs=[pl.BlockSpec(memory_space=pltpu.SMEM)]
        + [pl.BlockSpec(memory_space=pltpu.VMEM)] * len(pieces),
        out_specs=pl.BlockSpec(memory_space=pltpu.VMEM),
        out_shape=jax.ShapeDtypeStruct((n_b, n * NB), F32),
        name="place",
    )(c, *pieces)


def swap(x, axes, s):
    n = lax.axis_size(axes)
    return lax.ppermute(x, axes, [(i, i ^ s) for i in range(n)])


def gather(x, axes):
    got = [x]
    for s in range(1, lax.axis_size(axes)):
        got.append(swap(got[s & (s - 1)], axes, s & -s))
    return got


def pick(x, at):
    return lax.dynamic_index_in_dim(x, at, 0, keepdims=False)


def per_device(tokens, teacher, left_blocks, right_blocks):
    n_z = lax.axis_size("blk")
    n_c = lax.axis_size(("tok", "rep"))
    z = lax.axis_index("blk")
    c = lax.axis_index(("tok", "rep"))
    plane = ("tok", "rep")
    n_b = left_blocks.shape[0]
    n_k = teacher.shape[1] // FB
    n_q = n_k // GROUP
    scale = float(tokens.shape[0] * n_c) ** (-0.5)

    sides = right_blocks.reshape(n_q, 2, GROUP // 2, n_z, n_b, FB)
    perms = [
        [(a * n_c + b, (b ^ side) * n_c + a) for a in range(n_z) for b in range(n_c)] for side in (0, n_c // 2)
    ]
    sides = [lax.ppermute(sides[:, i], ("blk",) + plane, perm) for i, perm in enumerate(perms)]

    chips = [gather(own, "rep") for own in gather(tokens, "tok")]
    pieces = [p for chip in chips for p in chip]

    left = left_blocks.reshape(n_b * BI, NB)
    rows_kb = n_k * n_b
    take = (
        lax.broadcasted_iota(jnp.int32, (rows_kb, NB), 0) // n_b + c * n_k
        == lax.broadcasted_iota(jnp.int32, (rows_kb, NB), 1)
    ).astype(BF)
    diag = (
        lax.broadcasted_iota(jnp.int32, (rows_kb, n_b * BI), 0) % n_b
        == lax.broadcasted_iota(jnp.int32, (rows_kb, n_b * BI), 1) // BI
    )
    left = lax.dot_general(take, left, NT, preferred_element_type=F32)
    left = jnp.where(diag, left, 0.0).astype(BF)

    hid = [
        jnp.concatenate(
            [lax.dot_general(left, p, NT, preferred_element_type=F32).astype(BF) for p in chip], axis=1
        )
        for chip in chips
    ]
    hidden = list(zip(*[gather(h, "blk") for h in hid]))
    back, own = back_partial(jnp.reshape(z, (1,)).astype(jnp.int32), pieces, hid, teacher, sides, scale)
    backs = [back] + [swap(back[s], "blk", s) for s in range(1, n_z)]

    gl = grad_left_of(backs, pieces, n_k)
    gl = gl.reshape(n_k, n_b, n_c, BI // n_c).transpose(2, 0, 3, 1).reshape(n_c, n_k, -1)
    got = []
    for s in range(n_c):
        piece = pick(gl, c ^ s)
        got.append(swap(piece, plane, s) if s else piece)
    grad_left = place(jnp.reshape(c, (1,)).astype(jnp.int32), got, n_b)

    gr = grad_right_partial(pieces, teacher, hidden, own, scale)
    there = []
    for s in range(n_c):
        piece = pick(gr, z ^ c ^ s)
        there.append(swap(piece, plane, s) if s else piece)
    there = jnp.stack(there, 0)
    total = None
    for s in range(n_z):
        piece = pick(there, c ^ z ^ s)
        piece = (swap(piece, "blk", s) if s else piece).astype(F32)
        total = piece if total is None else total + piece
    grad_right = total.reshape(n_b, n_k, FB).transpose(1, 0, 2).reshape(n_k, n_b * FB)
    return grad_left, grad_right


def solution(mesh):
    return jax.shard_map(
        per_device,
        mesh=mesh,
        in_specs=(
            P(("layer", "tok", "rep"), "blk"),
            P(("layer", "blk"), ("tok", "rep")),
            P(("layer", "blk"), None),
            P(("layer", "blk"), None),
        ),
        out_specs=(P(("layer", "blk"), ("tok", "rep")), P(("layer", "blk"), ("tok", "rep"))),
        check_vma=False,
    )
```

```python
import functools

import jax
import jax.numpy as jnp
from jax import lax
from jax.experimental import pallas as pl
from jax.experimental.pallas import tpu as pltpu
from jax.sharding import PartitionSpec as P

D = 8192
F = 14336
NB = 64
BI = D // NB
FB = F // NB
GROUP = 4
COLS = GROUP * FB
BF = jnp.bfloat16
F32 = jnp.float32
NT = (((1,), (1,)), ((), ()))
TN = (((0,), (0,)), ((), ()))
SPLIT = 4
VMEM = 40 * 1024 * 1024


def cost(flops, nbytes):
    return pl.CostEstimate(flops=flops, bytes_accessed=nbytes, transcendentals=0)


def rows_of(refs):
    return jnp.concatenate([r[...] for r in refs], axis=0) if len(refs) > 1 else refs[0][...]


def spread(right):
    n_z, n_k, n_b, _ = right.shape
    rows = n_z * n_k * n_b
    col = lax.broadcasted_iota(jnp.int32, (1, COLS), 1)
    tile = (lax.broadcasted_iota(jnp.int32, (FB, 1), 0) == col % FB).astype(F32).astype(BF)
    wide = jnp.dot(right.reshape(rows, FB), tile, preferred_element_type=F32)
    k_row = lax.broadcasted_iota(jnp.int32, (rows, 1), 0) // n_b % n_k
    return jnp.where(k_row == col // FB, wide, 0.0).astype(BF)


def residual_kernel(scale, n_tok, n_hid, n_z, z_ref, *refs):
    tok_refs, refs = refs[:n_tok], refs[n_tok:]
    hid_refs, refs = refs[:n_hid], refs[n_hid:]
    teacher_refs, right_refs, (resid_ref, back_ref) = refs[:SPLIT], refs[SPLIT:-2], refs[-2:]
    right = jnp.stack(
        [jnp.concatenate([a[0, :, 0], b[0, :, 0]], axis=0) for a, b in zip(right_refs[:n_z], right_refs[n_z:])],
        axis=0,
    )
    right = spread(right)
    rows = right.shape[0] // n_z
    hid = jnp.concatenate([h[...] for h in hid_refs], axis=1)
    resid = lax.dot_general(hid, right[:rows], TN, preferred_element_type=F32) - jnp.dot(
        rows_of(tok_refs), rows_of(teacher_refs), preferred_element_type=F32
    )
    resid = (resid * scale).astype(BF)
    resid_ref[...] = resid
    back = lax.dot_general(right, resid, NT, preferred_element_type=F32)
    back_ref[...] = back.astype(BF).reshape(back_ref.shape)


def residual(z, tokens, hidden, teacher, sides, scale):
    piece, depth = tokens[0].shape
    t = piece * len(tokens)
    cols = teacher.shape[1]
    n_q, half, n_z, n_b, _ = sides[0].shape
    rows = GROUP * n_b
    right_specs = [
        pl.BlockSpec((1, half, 1, n_b, FB), lambda q, z, s=s: (q, 0, z[0] ^ s, 0, 0)) for s in range(n_z)
    ]
    return pl.pallas_call(
        functools.partial(residual_kernel, scale, len(tokens), len(hidden), n_z),
        grid_spec=pltpu.PrefetchScalarGridSpec(
            num_scalar_prefetch=1,
            grid=(n_q,),
            in_specs=[pl.BlockSpec((piece, depth), lambda q, z: (0, 0))] * len(tokens)
            + [pl.BlockSpec((rows, h.shape[1]), lambda q, z: (q, 0)) for h in hidden]
            + [pl.BlockSpec((depth // SPLIT, COLS), lambda q, z, i=i: (i, q)) for i in range(SPLIT)]
            + right_specs * 2,
            out_specs=[
                pl.BlockSpec((t, COLS), lambda q, z: (0, q)),
                pl.BlockSpec((n_z, rows, t), lambda q, z: (0, q, 0)),
            ],
        ),
        out_shape=[
            jax.ShapeDtypeStruct((t, cols), BF),
            jax.ShapeDtypeStruct((n_z, n_q * rows, t), BF),
        ],
        compiler_params=pltpu.CompilerParams(vmem_limit_bytes=VMEM),
        cost_estimate=cost(2 * t * cols * (depth + n_z * rows), 2 * depth * cols),
        name="residual",
    )(z, *tokens, *hidden, *[teacher] * SPLIT, *[sides[0]] * n_z, *[sides[1]] * n_z)


def grad_right_kernel(n_z, parts, *refs):
    hid_refs, (resid_ref, out_ref) = refs[:-2], refs[-2:]
    hid = jnp.concatenate(
        [
            jnp.concatenate([r[...] for r in hid_refs[s * parts : (s + 1) * parts]], axis=1)
            for s in range(n_z)
        ],
        axis=0,
    )
    prod = jnp.dot(hid, resid_ref[...], preferred_element_type=F32)
    prod = prod.reshape(n_z, GROUP, prod.shape[0] // (n_z * GROUP), COLS)
    block = lax.broadcasted_iota(jnp.int32, (1, 1, COLS), 2) // FB
    total = prod[:, 0]
    for k in range(1, GROUP):
        total = jnp.where(block == k, prod[:, k], total)
    out_ref[...] = total.astype(BF)


def grad_right_partial(hidden, resid):
    t, cols = resid.shape
    n_z, parts = len(hidden), len(hidden[0])
    n_q = cols // COLS
    rows = hidden[0][0].shape[0] // n_q
    return pl.pallas_call(
        functools.partial(grad_right_kernel, n_z, parts),
        grid=(n_q,),
        in_specs=[pl.BlockSpec((rows, h.shape[1]), lambda q: (q, 0)) for hs in hidden for h in hs]
        + [pl.BlockSpec((t, COLS), lambda q: (0, q))],
        out_specs=pl.BlockSpec((n_z, rows // GROUP, COLS), lambda q: (0, 0, q)),
        out_shape=jax.ShapeDtypeStruct((n_z, rows // GROUP, cols), BF),
        compiler_params=pltpu.CompilerParams(vmem_limit_bytes=VMEM),
        cost_estimate=cost(2 * t * cols * n_z * rows, 2 * t * cols),
        name="grad_right",
    )(*[h for hs in hidden for h in hs], resid)


def grad_left_kernel(n_z, n_k, *refs):
    back_refs, tok_refs, out_ref = refs[:n_z], refs[n_z:-1], refs[-1]
    total = back_refs[0][0].astype(F32)
    for ref in back_refs[1:]:
        total = total + ref[...].astype(F32)
    prod = jnp.dot(total.astype(BF), rows_of(tok_refs), preferred_element_type=F32)
    rows, block = prod.shape
    prod = prod.reshape(n_k, rows // n_k, block)
    at = pl.program_id(0) * (block // BI)
    own = lax.broadcasted_iota(jnp.int32, prod.shape, 1) == at + lax.broadcasted_iota(
        jnp.int32, prod.shape, 2
    ) // BI
    out_ref[...] = jnp.where(own, prod, 0.0).sum(1).astype(BF)


def grad_left_of(backs, tokens, n_k):
    n_z = len(backs)
    rows, t = backs[1].shape
    piece, depth = tokens[0].shape
    block = min(depth, 1024)
    return pl.pallas_call(
        functools.partial(grad_left_kernel, n_z, n_k),
        grid=(depth // block,),
        in_specs=[pl.BlockSpec((1, rows, t), lambda q: (0, 0, 0))]
        + [pl.BlockSpec((rows, t), lambda q: (0, 0))] * (n_z - 1)
        + [pl.BlockSpec((piece, block), lambda q: (0, q))] * len(tokens),
        out_specs=pl.BlockSpec((n_k, block), lambda q: (0, q)),
        out_shape=jax.ShapeDtypeStruct((n_k, depth), BF),
        compiler_params=pltpu.CompilerParams(vmem_limit_bytes=VMEM),
        cost_estimate=cost(2 * t * rows * depth, 2 * t * depth),
        name="grad_left",
    )(*backs, *tokens)


def place_kernel(n_b, c_ref, *refs):
    in_refs, out_ref = refs[:-1], refs[-1]
    n_c, n_k = len(in_refs), in_refs[0].shape[0]
    x = rows_of(in_refs)
    row = lax.broadcasted_iota(jnp.int32, (NB, NB), 0)
    col = lax.broadcasted_iota(jnp.int32, (NB, NB), 1)
    pick = row == ((col // n_k) ^ c_ref[0]) * n_k + col % n_k
    got = lax.dot_general(
        x, pick.astype(F32).astype(BF), (((0,), (1,)), ((), ())), preferred_element_type=F32
    )
    for j in range(got.shape[0] // n_b):
        out_ref[:, j * NB : (j + 1) * NB] = got[j * n_b : (j + 1) * n_b]


def place(c, pieces, n_b):
    n = pieces[0].shape[1] // n_b
    return pl.pallas_call(
        functools.partial(place_kernel, n_b),
        in_specs=[pl.BlockSpec(memory_space=pltpu.SMEM)]
        + [pl.BlockSpec(memory_space=pltpu.VMEM)] * len(pieces),
        out_specs=pl.BlockSpec(memory_space=pltpu.VMEM),
        out_shape=jax.ShapeDtypeStruct((n_b, n * NB), F32),
        name="place",
    )(c, *pieces)


def swap(x, axes, s):
    n = lax.axis_size(axes)
    return lax.ppermute(x, axes, [(i, i ^ s) for i in range(n)])


def gather(x, axes):
    got = [x]
    for s in range(1, lax.axis_size(axes)):
        got.append(swap(got[s & (s - 1)], axes, s & -s))
    return got


def pick(x, at):
    return lax.dynamic_index_in_dim(x, at, 0, keepdims=False)


def per_device(tokens, teacher, left_blocks, right_blocks):
    n_z = lax.axis_size("blk")
    n_tok = lax.axis_size("tok")
    n_c = lax.axis_size(("tok", "rep"))
    z = lax.axis_index("blk")
    c = lax.axis_index(("tok", "rep"))
    plane = ("tok", "rep")
    n_b = left_blocks.shape[0]
    n_k = teacher.shape[1] // FB
    n_q = n_k // GROUP
    scale = float(tokens.shape[0] * n_c) ** (-0.5)

    left = left_blocks.reshape(n_b * BI, NB)
    rows_kb = n_k * n_b
    take = (
        lax.broadcasted_iota(jnp.int32, (rows_kb, NB), 0) // n_b + c * n_k
        == lax.broadcasted_iota(jnp.int32, (rows_kb, NB), 1)
    ).astype(BF)
    diag = (
        lax.broadcasted_iota(jnp.int32, (rows_kb, n_b * BI), 0) % n_b
        == lax.broadcasted_iota(jnp.int32, (rows_kb, n_b * BI), 1) // BI
    )
    left = lax.dot_general(take, left, NT, preferred_element_type=F32)
    left = jnp.where(diag, left, 0.0).astype(BF)

    def hidden_of(chip):
        return jnp.concatenate(
            [lax.dot_general(left, p, NT, preferred_element_type=F32).astype(BF) for p in chip], axis=1
        )

    far = [swap(tokens, "tok", s) for s in range(1, n_tok)]
    near = gather(tokens, "rep")
    sides = right_blocks.reshape(n_q, 2, GROUP // 2, n_z, n_b, FB)
    turn = [
        [(a * n_c + b, (b ^ side) * n_c + a) for a in range(n_z) for b in range(n_c)] for side in (0, n_c // 2)
    ]
    sides = [lax.ppermute(sides[:, i], ("blk",) + plane, perm) for i, perm in enumerate(turn)]

    first = hidden_of(near)
    early = gather(first, "blk")
    far, early[1:], _ = lax.optimization_barrier((far, early[1:], sides))
    chips = [near] + [gather(x, "rep") for x in far]
    pieces = [p for chip in chips for p in chip]
    hid = [first] + [hidden_of(chip) for chip in chips[1:]]
    late = [[h] + [swap(h, "blk", s) for s in range(1, n_z)] for h in hid[1:]]
    hidden = list(zip(early, *late))
    resid, back = residual(jnp.reshape(z, (1,)).astype(jnp.int32), pieces, hid, teacher, sides, scale)
    backs = [back] + [swap(back[s], "blk", s) for s in range(1, n_z)]

    gl = grad_left_of(backs, pieces, n_k)
    gl = gl.reshape(n_k, n_b, n_c, BI // n_c).transpose(2, 0, 3, 1).reshape(n_c, n_k, -1)
    got = []
    for s in range(n_c):
        piece = pick(gl, c ^ s)
        got.append(swap(piece, plane, s) if s else piece)
    grad_left = place(jnp.reshape(c, (1,)).astype(jnp.int32), got, n_b)

    hidden[0], _ = lax.optimization_barrier((hidden[0], backs[1:]))
    gr = grad_right_partial(hidden, resid)
    total = gr[0].astype(F32)
    for s in range(1, n_z):
        total = total + swap(gr[s], "blk", s).astype(F32)
    total = lax.ppermute(total.astype(BF), ("blk",) + plane, turn[0])
    total = total.reshape(n_b, n_k, FB).transpose(1, 0, 2).reshape(n_k, n_b * FB)
    grad_right = total.astype(F32)
    return grad_left, grad_right


def solution(mesh):
    return jax.shard_map(
        per_device,
        mesh=mesh,
        in_specs=(
            P(("layer", "tok", "rep"), "blk"),
            P(("layer", "blk"), ("tok", "rep")),
            P(("layer", "blk"), None),
            P(("layer", "blk"), None),
        ),
        out_specs=(P(("layer", "blk"), ("tok", "rep")), P(("layer", "blk"), ("tok", "rep"))),
        check_vma=False,
    )
```

```python
import functools

import jax
import jax.numpy as jnp
from jax import lax
from jax.experimental import pallas as pl
from jax.experimental.pallas import tpu as pltpu
from jax.sharding import PartitionSpec as P

D = 8192
F = 14336
NB = 64
BI = D // NB
FB = F // NB
GROUP = 4
COLS = GROUP * FB
BF = jnp.bfloat16
F32 = jnp.float32
NT = (((1,), (1,)), ((), ()))
TN = (((0,), (0,)), ((), ()))
SPLIT = 4
VMEM = 40 * 1024 * 1024


def cost(flops, nbytes):
    return pl.CostEstimate(flops=flops, bytes_accessed=nbytes, transcendentals=0)


def rows_of(refs):
    return jnp.concatenate([r[...] for r in refs], axis=0) if len(refs) > 1 else refs[0][...]


def spread(right):
    n_z, n_k, n_b, _ = right.shape
    rows = n_z * n_k * n_b
    col = lax.broadcasted_iota(jnp.int32, (1, COLS), 1)
    tile = (lax.broadcasted_iota(jnp.int32, (FB, 1), 0) == col % FB).astype(F32).astype(BF)
    wide = jnp.dot(right.reshape(rows, FB), tile, preferred_element_type=F32)
    k_row = lax.broadcasted_iota(jnp.int32, (rows, 1), 0) // n_b % n_k
    return jnp.where(k_row == col // FB, wide, 0.0).astype(BF)


def target_kernel(pieces, *refs):
    tok_refs, teacher_refs, out_ref = refs[:pieces], refs[pieces:-1], refs[-1]
    out_ref[...] = jnp.dot(rows_of(tok_refs), rows_of(teacher_refs), preferred_element_type=F32).astype(BF)


def target(tokens, teacher):
    t, depth = tokens[0].shape
    cols = teacher.shape[1]
    block = 512 if cols % 512 == 0 else COLS
    total = t * len(tokens)
    return pl.pallas_call(
        functools.partial(target_kernel, len(tokens)),
        grid=(cols // block,),
        in_specs=[pl.BlockSpec((t, depth), lambda q: (0, 0))] * len(tokens)
        + [pl.BlockSpec((depth // SPLIT, block), lambda q, i=i: (i, q)) for i in range(SPLIT)],
        out_specs=pl.BlockSpec((total, block), lambda q: (0, q)),
        out_shape=jax.ShapeDtypeStruct((total, cols), BF),
        compiler_params=pltpu.CompilerParams(vmem_limit_bytes=VMEM),
        cost_estimate=cost(2 * total * cols * depth, 2 * depth * cols),
        name="target",
    )(*tokens, *[teacher] * SPLIT)


def project_kernel(scale, n_hid, n_z, z_ref, part_ref, *refs):
    hid_refs, right_refs, (resid_ref, back_ref) = refs[:n_hid], refs[n_hid:-2], refs[-2:]
    right = jnp.stack(
        [jnp.concatenate([a[0, :, 0], b[0, :, 0]], axis=0) for a, b in zip(right_refs[:n_z], right_refs[n_z:])],
        axis=0,
    )
    right = spread(right)
    rows = right.shape[0] // n_z
    hid = jnp.concatenate([h[...] for h in hid_refs], axis=1)
    student = lax.dot_general(hid, right[:rows], TN, preferred_element_type=F32)
    resid = ((student - part_ref[...].astype(F32)) * scale).astype(BF)
    resid_ref[...] = resid
    back = lax.dot_general(right, resid, NT, preferred_element_type=F32)
    back_ref[...] = back.astype(BF).reshape(back_ref.shape)


def project(z, part, hidden, sides, scale):
    t, cols = part.shape
    n_q, half, n_z, n_b, _ = sides[0].shape
    rows = GROUP * n_b
    right_specs = [
        pl.BlockSpec((1, half, 1, n_b, FB), lambda q, z, s=s: (q, 0, z[0] ^ s, 0, 0)) for s in range(n_z)
    ]
    return pl.pallas_call(
        functools.partial(project_kernel, scale, len(hidden), n_z),
        grid_spec=pltpu.PrefetchScalarGridSpec(
            num_scalar_prefetch=1,
            grid=(n_q,),
            in_specs=[pl.BlockSpec((t, COLS), lambda q, z: (0, q))]
            + [pl.BlockSpec((rows, h.shape[1]), lambda q, z: (q, 0)) for h in hidden]
            + right_specs * 2,
            out_specs=[
                pl.BlockSpec((t, COLS), lambda q, z: (0, q)),
                pl.BlockSpec((n_z, rows, t), lambda q, z: (0, q, 0)),
            ],
        ),
        out_shape=[
            jax.ShapeDtypeStruct((t, cols), BF),
            jax.ShapeDtypeStruct((n_z, n_q * rows, t), BF),
        ],
        compiler_params=pltpu.CompilerParams(vmem_limit_bytes=VMEM),
        cost_estimate=cost(2 * t * cols * n_z * rows * 2, 6 * t * cols),
        name="project",
    )(z, part, *hidden, *[sides[0]] * n_z, *[sides[1]] * n_z)


def grad_right_kernel(n_z, parts, *refs):
    hid_refs, (resid_ref, out_ref) = refs[:-2], refs[-2:]
    hid = jnp.concatenate(
        [
            jnp.concatenate([r[...] for r in hid_refs[s * parts : (s + 1) * parts]], axis=1)
            for s in range(n_z)
        ],
        axis=0,
    )
    prod = jnp.dot(hid, resid_ref[...], preferred_element_type=F32)
    prod = prod.reshape(n_z, GROUP, prod.shape[0] // (n_z * GROUP), COLS)
    block = lax.broadcasted_iota(jnp.int32, (1, 1, COLS), 2) // FB
    total = prod[:, 0]
    for k in range(1, GROUP):
        total = jnp.where(block == k, prod[:, k], total)
    out_ref[...] = total.astype(BF)


def grad_right_partial(hidden, resid):
    t, cols = resid.shape
    n_z, parts = len(hidden), len(hidden[0])
    n_q = cols // COLS
    rows = hidden[0][0].shape[0] // n_q
    return pl.pallas_call(
        functools.partial(grad_right_kernel, n_z, parts),
        grid=(n_q,),
        in_specs=[pl.BlockSpec((rows, h.shape[1]), lambda q: (q, 0)) for hs in hidden for h in hs]
        + [pl.BlockSpec((t, COLS), lambda q: (0, q))],
        out_specs=pl.BlockSpec((n_z, rows // GROUP, COLS), lambda q: (0, 0, q)),
        out_shape=jax.ShapeDtypeStruct((n_z, rows // GROUP, cols), BF),
        compiler_params=pltpu.CompilerParams(vmem_limit_bytes=VMEM),
        cost_estimate=cost(2 * t * cols * n_z * rows, 2 * t * cols),
        name="grad_right",
    )(*[h for hs in hidden for h in hs], resid)


def grad_left_kernel(n_z, n_k, *refs):
    back_refs, tok_refs, out_ref = refs[:n_z], refs[n_z:-1], refs[-1]
    total = back_refs[0][0].astype(F32)
    for ref in back_refs[1:]:
        total = total + ref[...].astype(F32)
    prod = jnp.dot(total.astype(BF), rows_of(tok_refs), preferred_element_type=F32)
    rows, block = prod.shape
    prod = prod.reshape(n_k, rows // n_k, block)
    at = pl.program_id(0) * (block // BI)
    own = lax.broadcasted_iota(jnp.int32, prod.shape, 1) == at + lax.broadcasted_iota(
        jnp.int32, prod.shape, 2
    ) // BI
    out_ref[...] = jnp.where(own, prod, 0.0).sum(1).astype(BF)


def grad_left_of(backs, tokens, n_k):
    n_z = len(backs)
    rows, t = backs[1].shape
    piece, depth = tokens[0].shape
    block = min(depth, 1024)
    return pl.pallas_call(
        functools.partial(grad_left_kernel, n_z, n_k),
        grid=(depth // block,),
        in_specs=[pl.BlockSpec((1, rows, t), lambda q: (0, 0, 0))]
        + [pl.BlockSpec((rows, t), lambda q: (0, 0))] * (n_z - 1)
        + [pl.BlockSpec((piece, block), lambda q: (0, q))] * len(tokens),
        out_specs=pl.BlockSpec((n_k, block), lambda q: (0, q)),
        out_shape=jax.ShapeDtypeStruct((n_k, depth), BF),
        compiler_params=pltpu.CompilerParams(vmem_limit_bytes=VMEM),
        cost_estimate=cost(2 * t * rows * depth, 2 * t * depth),
        name="grad_left",
    )(*backs, *tokens)


def place_kernel(n_b, c_ref, *refs):
    in_refs, out_ref = refs[:-1], refs[-1]
    n_c, n_k = len(in_refs), in_refs[0].shape[0]
    x = rows_of(in_refs)
    row = lax.broadcasted_iota(jnp.int32, (NB, NB), 0)
    col = lax.broadcasted_iota(jnp.int32, (NB, NB), 1)
    pick = row == ((col // n_k) ^ c_ref[0]) * n_k + col % n_k
    got = lax.dot_general(
        x, pick.astype(F32).astype(BF), (((0,), (1,)), ((), ())), preferred_element_type=F32
    )
    for j in range(got.shape[0] // n_b):
        out_ref[:, j * NB : (j + 1) * NB] = got[j * n_b : (j + 1) * n_b]


def place(c, pieces, n_b):
    n = pieces[0].shape[1] // n_b
    return pl.pallas_call(
        functools.partial(place_kernel, n_b),
        in_specs=[pl.BlockSpec(memory_space=pltpu.SMEM)]
        + [pl.BlockSpec(memory_space=pltpu.VMEM)] * len(pieces),
        out_specs=pl.BlockSpec(memory_space=pltpu.VMEM),
        out_shape=jax.ShapeDtypeStruct((n_b, n * NB), F32),
        name="place",
    )(c, *pieces)


def swap(x, axes, s):
    n = lax.axis_size(axes)
    return lax.ppermute(x, axes, [(i, i ^ s) for i in range(n)])


def gather(x, axes):
    got = [x]
    for s in range(1, lax.axis_size(axes)):
        got.append(swap(got[s & (s - 1)], axes, s & -s))
    return got


def pick(x, at):
    return lax.dynamic_index_in_dim(x, at, 0, keepdims=False)


def per_device(tokens, teacher, left_blocks, right_blocks):
    n_z = lax.axis_size("blk")
    n_tok = lax.axis_size("tok")
    n_c = lax.axis_size(("tok", "rep"))
    z = lax.axis_index("blk")
    c = lax.axis_index(("tok", "rep"))
    plane = ("tok", "rep")
    n_b = left_blocks.shape[0]
    n_k = teacher.shape[1] // FB
    n_q = n_k // GROUP
    scale = float(tokens.shape[0] * n_c) ** (-0.5)

    left = left_blocks.reshape(n_b * BI, NB)
    rows_kb = n_k * n_b
    take = (
        lax.broadcasted_iota(jnp.int32, (rows_kb, NB), 0) // n_b + c * n_k
        == lax.broadcasted_iota(jnp.int32, (rows_kb, NB), 1)
    ).astype(BF)
    diag = (
        lax.broadcasted_iota(jnp.int32, (rows_kb, n_b * BI), 0) % n_b
        == lax.broadcasted_iota(jnp.int32, (rows_kb, n_b * BI), 1) // BI
    )
    left = lax.dot_general(take, left, NT, preferred_element_type=F32)
    left = jnp.where(diag, left, 0.0).astype(BF)

    def hidden_of(chip):
        return jnp.concatenate(
            [lax.dot_general(left, p, NT, preferred_element_type=F32).astype(BF) for p in chip], axis=1
        )

    far = [swap(tokens, "tok", s) for s in range(1, n_tok)]
    near = gather(tokens, "rep")
    first = hidden_of(near)
    early = gather(first, "blk")
    sides = right_blocks.reshape(n_q, 2, GROUP // 2, n_z, n_b, FB)
    sides = [sides[:, i] for i in range(2)]
    far, early[1:3], sides = lax.optimization_barrier((far, early[1:3], sides))

    turn = [
        [(a * n_c + b, (b ^ side) * n_c + a) for a in range(n_z) for b in range(n_c)] for side in (0, n_c // 2)
    ]
    sides = [lax.ppermute(x, ("blk",) + plane, perm) for x, perm in zip(sides, turn)]

    chips = [near] + [gather(x, "rep") for x in far]
    pieces = [p for chip in chips for p in chip]
    hid = [first] + [hidden_of(chip) for chip in chips[1:]]
    late = [[swap(h, "blk", s) for s in range(1, n_z)] for h in hid[1:]]
    part, late, sides = lax.optimization_barrier((target(pieces, teacher), late, sides))
    resid, back = project(jnp.reshape(z, (1,)).astype(jnp.int32), part, hid, sides, scale)
    backs = [back] + [swap(back[s], "blk", s) for s in range(1, n_z)]
    hidden = list(zip(early, *[[h] + x for h, x in zip(hid[1:], late)]))

    gr = grad_right_partial(hidden, resid)
    total = gr[0].astype(F32)
    for s in range(1, n_z):
        total = total + swap(gr[s], "blk", s).astype(F32)
    total = lax.ppermute(total.astype(BF), ("blk",) + plane, turn[0])
    grad_right = total.reshape(n_b, n_k, FB).transpose(1, 0, 2).reshape(n_k, n_b * FB).astype(F32)

    gl = grad_left_of(backs, pieces, n_k)
    gl = gl.reshape(n_k, n_b, n_c, BI // n_c).transpose(2, 0, 3, 1).reshape(n_c, n_k, -1)
    got = []
    for s in range(n_c):
        piece = pick(gl, c ^ s)
        got.append(swap(piece, plane, s) if s else piece)
    grad_left = place(jnp.reshape(c, (1,)).astype(jnp.int32), got, n_b)

    return grad_left, grad_right


def solution(mesh):
    return jax.shard_map(
        per_device,
        mesh=mesh,
        in_specs=(
            P(("layer", "tok", "rep"), "blk"),
            P(("layer", "blk"), ("tok", "rep")),
            P(("layer", "blk"), None),
            P(("layer", "blk"), None),
        ),
        out_specs=(P(("layer", "blk"), ("tok", "rep")), P(("layer", "blk"), ("tok", "rep"))),
        check_vma=False,
    )
```

```python
import functools

import jax
import jax.numpy as jnp
from jax import lax
from jax.experimental import pallas as pl
from jax.experimental.pallas import tpu as pltpu
from jax.sharding import PartitionSpec as P

D = 8192
F = 14336
NB = 64
BI = D // NB
FB = F // NB
GROUP = 4
COLS = GROUP * FB
BF = jnp.bfloat16
F32 = jnp.float32
NT = (((1,), (1,)), ((), ()))
TN = (((0,), (0,)), ((), ()))
SPLIT = 4
VMEM = 40 * 1024 * 1024


def cost(flops, nbytes):
    return pl.CostEstimate(flops=flops, bytes_accessed=nbytes, transcendentals=0)


def rows_of(refs):
    return jnp.concatenate([r[...] for r in refs], axis=0) if len(refs) > 1 else refs[0][...]


def spread(right):
    n_z, n_k, n_b, _ = right.shape
    rows = n_z * n_k * n_b
    col = lax.broadcasted_iota(jnp.int32, (1, COLS), 1)
    tile = (lax.broadcasted_iota(jnp.int32, (FB, 1), 0) == col % FB).astype(F32).astype(BF)
    wide = jnp.dot(right.reshape(rows, FB), tile, preferred_element_type=F32)
    k_row = lax.broadcasted_iota(jnp.int32, (rows, 1), 0) // n_b % n_k
    return jnp.where(k_row == col // FB, wide, 0.0).astype(BF)


def target_kernel(pieces, *refs):
    tok_refs, teacher_refs, out_ref = refs[:pieces], refs[pieces:-1], refs[-1]
    out_ref[...] = jnp.dot(rows_of(tok_refs), rows_of(teacher_refs), preferred_element_type=F32).astype(BF)


def target(tokens, teacher):
    t, depth = tokens[0].shape
    cols = teacher.shape[1]
    block = 512 if cols % 512 == 0 else COLS
    total = t * len(tokens)
    return pl.pallas_call(
        functools.partial(target_kernel, len(tokens)),
        grid=(cols // block,),
        in_specs=[pl.BlockSpec((t, depth), lambda q: (0, 0))] * len(tokens)
        + [pl.BlockSpec((depth // SPLIT, block), lambda q, i=i: (i, q)) for i in range(SPLIT)],
        out_specs=pl.BlockSpec((total, block), lambda q: (0, q)),
        out_shape=jax.ShapeDtypeStruct((total, cols), BF),
        compiler_params=pltpu.CompilerParams(vmem_limit_bytes=VMEM),
        cost_estimate=cost(2 * total * cols * depth, 2 * depth * cols),
        name="target",
    )(*tokens, *[teacher] * SPLIT)


def project_kernel(scale, n_hid, n_z, n_per, z_ref, part_ref, *refs):
    hid_refs, right_refs, (resid_ref, back_ref) = refs[:n_hid], refs[n_hid:-2], refs[-2:]
    right = jnp.stack([r[0, :, 0] for r in right_refs[:n_z]], axis=0)
    if len(right_refs) > n_z:
        other = jnp.stack([r[0, :, 0] for r in right_refs[n_z:]], axis=0)
        right = jnp.where(pl.program_id(0) < n_per, right, other)
    right = spread(right)
    rows = right.shape[0] // n_z
    hid = jnp.concatenate([h[...] for h in hid_refs], axis=1)
    student = lax.dot_general(hid, right[:rows], TN, preferred_element_type=F32)
    resid = ((student - part_ref[...].astype(F32)) * scale).astype(BF)
    resid_ref[...] = resid
    back = lax.dot_general(right, resid, NT, preferred_element_type=F32)
    back_ref[...] = back.astype(BF).reshape(back_ref.shape)


def project(z, part, hidden, sides, scale):
    t, cols = part.shape
    n_per, _, n_z, n_b, _ = sides[0].shape
    n_q = n_per * len(sides)
    rows = GROUP * n_b

    def at(q, i):
        return jnp.clip(q - i * n_per, 0, n_per - 1)

    right_specs = [
        pl.BlockSpec((1, GROUP, 1, n_b, FB), lambda q, z, s=s, i=i: (at(q, i), 0, z[0] ^ s, 0, 0))
        for i in range(len(sides))
        for s in order_of(n_z)
    ]
    return pl.pallas_call(
        functools.partial(project_kernel, scale, len(hidden), n_z, n_per),
        grid_spec=pltpu.PrefetchScalarGridSpec(
            num_scalar_prefetch=1,
            grid=(n_q,),
            in_specs=[pl.BlockSpec((t, COLS), lambda q, z: (0, q))]
            + [pl.BlockSpec((rows, h.shape[1]), lambda q, z: (q, 0)) for h in hidden]
            + right_specs,
            out_specs=[
                pl.BlockSpec((t, COLS), lambda q, z: (0, q)),
                pl.BlockSpec((n_z, rows, t), lambda q, z: (0, q, 0)),
            ],
        ),
        out_shape=[
            jax.ShapeDtypeStruct((t, cols), BF),
            jax.ShapeDtypeStruct((n_z, n_q * rows, t), BF),
        ],
        compiler_params=pltpu.CompilerParams(vmem_limit_bytes=VMEM),
        cost_estimate=cost(2 * t * cols * n_z * rows * 2, 6 * t * cols),
        name="project",
    )(z, part, *hidden, *[x for x in sides for _ in range(n_z)])


def grad_right_kernel(*refs):
    hid_refs, (resid_ref, first_ref, second_ref) = refs[:-3], refs[-3:]
    hid = jnp.concatenate(
        [jnp.concatenate([r[...] for r in hid_refs[h::2]], axis=2) for h in range(2)], axis=0
    )
    n_z, rows, t = hid.shape
    prod = jnp.dot(hid.reshape(n_z * rows, t), resid_ref[...], preferred_element_type=F32)
    prod = prod.reshape(n_z, GROUP, rows // GROUP, COLS)
    block = lax.broadcasted_iota(jnp.int32, (1, 1, COLS), 2) // FB
    total = prod[:, 0]
    for k in range(1, GROUP):
        total = jnp.where(block == k, prod[:, k], total)
    first_ref[...] = total[: n_z // 2].astype(BF)
    second_ref[...] = total[n_z // 2 :].astype(BF)


def grad_right_partial(hidden, resid):
    t, cols = resid.shape
    n_q = cols // COLS
    half, rows, _ = hidden[0][0].shape
    rows //= n_q
    return pl.pallas_call(
        grad_right_kernel,
        grid=(n_q,),
        in_specs=[
            pl.BlockSpec((half, rows, h.shape[2]), lambda q: (0, q, 0)) for hs in hidden for h in hs
        ]
        + [pl.BlockSpec((t, COLS), lambda q: (0, q))],
        out_specs=[pl.BlockSpec((half, rows // GROUP, COLS), lambda q: (0, 0, q))] * 2,
        out_shape=[jax.ShapeDtypeStruct((half, rows // GROUP, cols), BF)] * 2,
        compiler_params=pltpu.CompilerParams(vmem_limit_bytes=VMEM),
        cost_estimate=cost(4 * t * cols * half * rows, 2 * t * cols),
        name="grad_right",
    )(*[h for hs in hidden for h in hs], resid)


def grad_left_kernel(n_z, n_k, *refs):
    back_refs, tok_refs, out_ref = refs[:n_z], refs[n_z:-1], refs[-1]
    total = back_refs[0][0].astype(F32)
    for ref in back_refs[1:]:
        total = total + ref[...].astype(F32)
    prod = jnp.dot(total.astype(BF), rows_of(tok_refs), preferred_element_type=F32)
    rows, block = prod.shape
    prod = prod.reshape(n_k, rows // n_k, block)
    at = pl.program_id(0) * (block // BI)
    own = lax.broadcasted_iota(jnp.int32, prod.shape, 1) == at + lax.broadcasted_iota(
        jnp.int32, prod.shape, 2
    ) // BI
    out_ref[...] = jnp.where(own, prod, 0.0).sum(1).astype(BF)


def grad_left_of(backs, tokens, n_k):
    n_z = len(backs)
    rows, t = backs[1].shape
    piece, depth = tokens[0].shape
    block = min(depth, 1024)
    return pl.pallas_call(
        functools.partial(grad_left_kernel, n_z, n_k),
        grid=(depth // block,),
        in_specs=[pl.BlockSpec((1, rows, t), lambda q: (0, 0, 0))]
        + [pl.BlockSpec((rows, t), lambda q: (0, 0))] * (n_z - 1)
        + [pl.BlockSpec((piece, block), lambda q: (0, q))] * len(tokens),
        out_specs=pl.BlockSpec((n_k, block), lambda q: (0, q)),
        out_shape=jax.ShapeDtypeStruct((n_k, depth), BF),
        compiler_params=pltpu.CompilerParams(vmem_limit_bytes=VMEM),
        cost_estimate=cost(2 * t * rows * depth, 2 * t * depth),
        name="grad_left",
    )(*backs, *tokens)


def place_kernel(n_b, c_ref, *refs):
    in_refs, out_ref = refs[:-1], refs[-1]
    n_c, n_k = len(in_refs), in_refs[0].shape[0]
    x = rows_of(in_refs)
    row = lax.broadcasted_iota(jnp.int32, (NB, NB), 0)
    col = lax.broadcasted_iota(jnp.int32, (NB, NB), 1)
    pick = row == ((col // n_k) ^ c_ref[0]) * n_k + col % n_k
    got = lax.dot_general(
        x, pick.astype(F32).astype(BF), (((0,), (1,)), ((), ())), preferred_element_type=F32
    )
    for j in range(got.shape[0] // n_b):
        out_ref[:, j * NB : (j + 1) * NB] = got[j * n_b : (j + 1) * n_b]


def place(c, pieces, n_b):
    n = pieces[0].shape[1] // n_b
    return pl.pallas_call(
        functools.partial(place_kernel, n_b),
        in_specs=[pl.BlockSpec(memory_space=pltpu.SMEM)]
        + [pl.BlockSpec(memory_space=pltpu.VMEM)] * len(pieces),
        out_specs=pl.BlockSpec(memory_space=pltpu.VMEM),
        out_shape=jax.ShapeDtypeStruct((n_b, n * NB), F32),
        name="place",
    )(c, *pieces)


def swap(x, axes, s):
    n = lax.axis_size(axes)
    return lax.ppermute(x, axes, [(i, i ^ s) for i in range(n)])


def gather(x, axes):
    got = [x]
    for s in range(1, lax.axis_size(axes)):
        got.append(swap(got[s & (s - 1)], axes, s & -s))
    return got


def doubling(x, axes, second):
    bit = lax.axis_size(axes) // 4
    first, second = x[None], second[None]
    while bit:
        if second is not None:
            first = jnp.concatenate([first, second], axis=0)
        second = swap(first, axes, bit)
        bit //= 2
    return first, second


def order_of(n):
    order, bit = [0], n // 2
    while bit:
        order, bit = order + [o ^ bit for o in order], bit // 2
    return order


def pick(x, at):
    return lax.dynamic_index_in_dim(x, at, 0, keepdims=False)


def per_device(tokens, teacher, left_blocks, right_blocks):
    n_z = lax.axis_size("blk")
    n_tok = lax.axis_size("tok")
    n_c = lax.axis_size(("tok", "rep"))
    z = lax.axis_index("blk")
    c = lax.axis_index(("tok", "rep"))
    plane = ("tok", "rep")
    n_b = left_blocks.shape[0]
    n_k = teacher.shape[1] // FB
    n_q = n_k // GROUP
    scale = float(tokens.shape[0] * n_c) ** (-0.5)

    left = left_blocks.reshape(n_b * BI, NB)
    rows_kb = n_k * n_b
    take = (
        lax.broadcasted_iota(jnp.int32, (rows_kb, NB), 0) // n_b + c * n_k
        == lax.broadcasted_iota(jnp.int32, (rows_kb, NB), 1)
    ).astype(BF)
    diag = (
        lax.broadcasted_iota(jnp.int32, (rows_kb, n_b * BI), 0) % n_b
        == lax.broadcasted_iota(jnp.int32, (rows_kb, n_b * BI), 1) // BI
    )
    left = lax.dot_general(take, left, NT, preferred_element_type=F32)
    left = jnp.where(diag, left, 0.0).astype(BF)

    def hidden_of(chip):
        return jnp.concatenate(
            [lax.dot_general(left, p, NT, preferred_element_type=F32).astype(BF) for p in chip], axis=1
        )

    turn = [
        [(a * n_c + b, (b ^ side) * n_c + a) for a in range(n_z) for b in range(n_c)] for side in (0, n_c // 2)
    ]
    n_side = 2 if n_q % 2 == 0 else 1
    sides = [
        lax.ppermute(x, ("blk",) + plane, perm).reshape(n_q // n_side, GROUP, n_z, n_b, FB)
        for x, perm in zip(jnp.split(right_blocks, n_side), turn)
    ]

    far = [swap(tokens, "tok", s) for s in range(1, n_tok)]
    near = gather(tokens, "rep")
    first = hidden_of(near)
    early = doubling(first, "blk", swap(first, "blk", n_z // 2))
    far, _, _ = lax.optimization_barrier((far, early[0], sides))
    chips = [near] + [gather(x, "rep") for x in far]
    pieces = [p for chip in chips for p in chip]
    hid = [first] + [hidden_of(chip) for chip in chips[1:]]
    late = [swap(h, "blk", n_z // 2) for h in hid[1:]]
    part, late = lax.optimization_barrier((target(pieces, teacher), late))
    late = [doubling(h, "blk", x) for h, x in zip(hid[1:], late)]
    resid, back = project(jnp.reshape(z, (1,)).astype(jnp.int32), part, hid, sides, scale)
    backs = [back] + [swap(back[i], "blk", s) for i, s in enumerate(order_of(n_z)) if s]

    mine, others = grad_right_partial([early] + late, resid)
    bit = 1
    while True:
        mine = mine.astype(F32) + swap(others, "blk", bit).astype(F32)
        if mine.shape[0] == 1:
            break
        mine = mine.astype(BF)
        mine, others = mine[: mine.shape[0] // 2], mine[mine.shape[0] // 2 :]
        bit *= 2
    total = lax.ppermute(mine[0].astype(BF), ("blk",) + plane, turn[0])
    grad_right = total.reshape(n_b, n_k, FB).transpose(1, 0, 2).reshape(n_k, n_b * FB).astype(F32)

    gl = grad_left_of(backs, pieces, n_k)
    gl = gl.reshape(n_k, n_b, n_c, BI // n_c).transpose(2, 0, 3, 1).reshape(n_c, n_k, -1)
    got = []
    for s in range(n_c):
        piece = pick(gl, c ^ s)
        got.append(swap(piece, plane, s) if s else piece)
    grad_left = place(jnp.reshape(c, (1,)).astype(jnp.int32), got, n_b)

    return grad_left, grad_right


def solution(mesh):
    return jax.shard_map(
        per_device,
        mesh=mesh,
        in_specs=(
            P(("layer", "tok", "rep"), "blk"),
            P(("layer", "blk"), ("tok", "rep")),
            P(("layer", "blk"), None),
            P(("layer", "blk"), None),
        ),
        out_specs=(P(("layer", "blk"), ("tok", "rep")), P(("layer", "blk"), ("tok", "rep"))),
        check_vma=False,
    )
```

```python
import functools

import jax
import jax.numpy as jnp
from jax import lax
from jax.experimental import pallas as pl
from jax.experimental.pallas import tpu as pltpu
from jax.sharding import PartitionSpec as P

D = 8192
F = 14336
NB = 64
BI = D // NB
FB = F // NB
GROUP = 4
COLS = GROUP * FB
BF = jnp.bfloat16
F32 = jnp.float32
NT = (((1,), (1,)), ((), ()))
TN = (((0,), (0,)), ((), ()))
SPLIT = 4
VMEM = 40 * 1024 * 1024


def cost(flops, nbytes):
    return pl.CostEstimate(flops=flops, bytes_accessed=nbytes, transcendentals=0)


def rows_of(refs):
    return jnp.concatenate([r[...] for r in refs], axis=0) if len(refs) > 1 else refs[0][...]


def spread(right):
    n_z, n_k, n_b, _ = right.shape
    rows = n_z * n_k * n_b
    col = lax.broadcasted_iota(jnp.int32, (1, COLS), 1)
    tile = (lax.broadcasted_iota(jnp.int32, (FB, 1), 0) == col % FB).astype(F32).astype(BF)
    wide = jnp.dot(right.reshape(rows, FB), tile, preferred_element_type=F32)
    k_row = lax.broadcasted_iota(jnp.int32, (rows, 1), 0) // n_b % n_k
    return jnp.where(k_row == col // FB, wide, 0.0).astype(BF)


def target_kernel(pieces, *refs):
    tok_refs, teacher_refs, out_ref = refs[:pieces], refs[pieces:-1], refs[-1]
    out_ref[...] = jnp.dot(rows_of(tok_refs), rows_of(teacher_refs), preferred_element_type=F32).astype(BF)


def target(tokens, teacher):
    t, depth = tokens[0].shape
    cols = teacher.shape[1]
    block = 512 if cols % 512 == 0 else COLS
    total = t * len(tokens)
    return pl.pallas_call(
        functools.partial(target_kernel, len(tokens)),
        grid=(cols // block,),
        in_specs=[pl.BlockSpec((t, depth), lambda q: (0, 0))] * len(tokens)
        + [pl.BlockSpec((depth // SPLIT, block), lambda q, i=i: (i, q)) for i in range(SPLIT)],
        out_specs=pl.BlockSpec((total, block), lambda q: (0, q)),
        out_shape=jax.ShapeDtypeStruct((total, cols), BF),
        compiler_params=pltpu.CompilerParams(vmem_limit_bytes=VMEM),
        cost_estimate=cost(2 * total * cols * depth, 2 * depth * cols),
        name="target",
    )(*tokens, *[teacher] * SPLIT)


def project_kernel(scale, n_hid, z_ref, part_ref, *refs):
    hid_refs, right_refs, (resid_ref, back_ref) = refs[:n_hid], refs[n_hid:-2], refs[-2:]
    right = spread(jnp.stack([r[0, :, 0] for r in right_refs], axis=0))
    rows = right.shape[0] // len(right_refs)
    hid = jnp.concatenate([h[...] for h in hid_refs], axis=1)
    student = lax.dot_general(hid, right[:rows], TN, preferred_element_type=F32)
    resid = ((student - part_ref[...].astype(F32)) * scale).astype(BF)
    resid_ref[...] = resid
    back = lax.dot_general(right, resid, NT, preferred_element_type=F32)
    back_ref[...] = back.astype(BF).reshape(back_ref.shape)


def project(z, part, hidden, right, scale):
    t, cols = part.shape
    n_q, _, n_z, n_b, _ = right.shape
    rows = GROUP * n_b
    right_specs = [
        pl.BlockSpec((1, GROUP, 1, n_b, FB), lambda q, z, s=s: (q, 0, z[0] ^ s, 0, 0)) for s in order_of(n_z)
    ]
    return pl.pallas_call(
        functools.partial(project_kernel, scale, len(hidden)),
        grid_spec=pltpu.PrefetchScalarGridSpec(
            num_scalar_prefetch=1,
            grid=(n_q,),
            in_specs=[pl.BlockSpec((t, COLS), lambda q, z: (0, q))]
            + [pl.BlockSpec((rows, h.shape[1]), lambda q, z: (q, 0)) for h in hidden]
            + right_specs,
            out_specs=[
                pl.BlockSpec((t, COLS), lambda q, z: (0, q)),
                pl.BlockSpec((n_z, rows, t), lambda q, z: (0, q, 0)),
            ],
        ),
        out_shape=[
            jax.ShapeDtypeStruct((t, cols), BF),
            jax.ShapeDtypeStruct((n_z, n_q * rows, t), BF),
        ],
        compiler_params=pltpu.CompilerParams(vmem_limit_bytes=VMEM),
        cost_estimate=cost(1, 1),
        name="project",
    )(z, part, *hidden, *[right] * n_z)


def grad_right_kernel(n_z, parts, *refs):
    hid_refs, (resid_ref, first_ref, second_ref) = refs[:-3], refs[-3:]
    hid = jnp.concatenate(
        [
            jnp.concatenate([r[...] for r in hid_refs[s * parts : (s + 1) * parts]], axis=1)
            for s in range(n_z)
        ],
        axis=0,
    )
    prod = jnp.dot(hid, resid_ref[...], preferred_element_type=F32)
    prod = prod.reshape(n_z, GROUP, prod.shape[0] // (n_z * GROUP), COLS)
    block = lax.broadcasted_iota(jnp.int32, (1, 1, COLS), 2) // FB
    total = prod[:, 0]
    for k in range(1, GROUP):
        total = jnp.where(block == k, prod[:, k], total)
    first_ref[...] = total[: n_z // 2].astype(BF)
    second_ref[...] = total[n_z // 2 :].astype(BF)


def grad_right_partial(hidden, resid):
    t, cols = resid.shape
    n_z, parts = len(hidden), len(hidden[0])
    n_q = cols // COLS
    rows = hidden[0][0].shape[0] // n_q
    return pl.pallas_call(
        functools.partial(grad_right_kernel, n_z, parts),
        grid=(n_q,),
        in_specs=[pl.BlockSpec((rows, h.shape[1]), lambda q: (q, 0)) for hs in hidden for h in hs]
        + [pl.BlockSpec((t, COLS), lambda q: (0, q))],
        out_specs=[pl.BlockSpec((n_z // 2, rows // GROUP, COLS), lambda q: (0, 0, q))] * 2,
        out_shape=[jax.ShapeDtypeStruct((n_z // 2, rows // GROUP, cols), BF)] * 2,
        compiler_params=pltpu.CompilerParams(vmem_limit_bytes=VMEM),
        cost_estimate=cost(2 * t * cols * n_z * rows, 2 * t * cols),
        name="grad_right",
    )(*[h for hs in hidden for h in hs], resid)


def grad_left_kernel(n_z, n_k, *refs):
    back_refs, tok_refs, out_ref = refs[:n_z], refs[n_z:-1], refs[-1]
    total = back_refs[0][0].astype(F32)
    for ref in back_refs[1:]:
        total = total + ref[...].astype(F32)
    prod = jnp.dot(total.astype(BF), rows_of(tok_refs), preferred_element_type=F32)
    rows, block = prod.shape
    prod = prod.reshape(n_k, rows // n_k, block)
    at = pl.program_id(0) * (block // BI)
    own = lax.broadcasted_iota(jnp.int32, prod.shape, 1) == at + lax.broadcasted_iota(
        jnp.int32, prod.shape, 2
    ) // BI
    out_ref[...] = jnp.where(own, prod, 0.0).sum(1).astype(BF)


def grad_left_of(backs, tokens, n_k):
    n_z = len(backs)
    rows, t = backs[1].shape
    piece, depth = tokens[0].shape
    block = min(depth, 1024)
    return pl.pallas_call(
        functools.partial(grad_left_kernel, n_z, n_k),
        grid=(depth // block,),
        in_specs=[pl.BlockSpec((1, rows, t), lambda q: (0, 0, 0))]
        + [pl.BlockSpec((rows, t), lambda q: (0, 0))] * (n_z - 1)
        + [pl.BlockSpec((piece, block), lambda q: (0, q))] * len(tokens),
        out_specs=pl.BlockSpec((n_k, block), lambda q: (0, q)),
        out_shape=jax.ShapeDtypeStruct((n_k, depth), BF),
        compiler_params=pltpu.CompilerParams(vmem_limit_bytes=VMEM),
        cost_estimate=cost(2 * t * rows * depth, 2 * t * depth),
        name="grad_left",
    )(*backs, *tokens)


def place_kernel(n_b, c_ref, *refs):
    in_refs, out_ref = refs[:-1], refs[-1]
    n_c, n_k = len(in_refs), in_refs[0].shape[0]
    x = rows_of(in_refs)
    row = lax.broadcasted_iota(jnp.int32, (NB, NB), 0)
    col = lax.broadcasted_iota(jnp.int32, (NB, NB), 1)
    pick = row == ((col // n_k) ^ c_ref[0]) * n_k + col % n_k
    got = lax.dot_general(
        x, pick.astype(F32).astype(BF), (((0,), (1,)), ((), ())), preferred_element_type=F32
    )
    for j in range(got.shape[0] // n_b):
        out_ref[:, j * NB : (j + 1) * NB] = got[j * n_b : (j + 1) * n_b]


def place(c, pieces, n_b):
    n = pieces[0].shape[1] // n_b
    return pl.pallas_call(
        functools.partial(place_kernel, n_b),
        in_specs=[pl.BlockSpec(memory_space=pltpu.SMEM)]
        + [pl.BlockSpec(memory_space=pltpu.VMEM)] * len(pieces),
        out_specs=pl.BlockSpec(memory_space=pltpu.VMEM),
        out_shape=jax.ShapeDtypeStruct((n_b, n * NB), F32),
        name="place",
    )(c, *pieces)


def swap(x, axes, s):
    n = lax.axis_size(axes)
    return lax.ppermute(x, axes, [(i, i ^ s) for i in range(n)])


def gather(x, axes):
    got = [x]
    for s in range(1, lax.axis_size(axes)):
        got.append(swap(got[s & (s - 1)], axes, s & -s))
    return got


def order_of(n):
    order, bit = [0], n // 2
    while bit:
        order, bit = order + [o ^ bit for o in order], bit // 2
    return order


def pick(x, at):
    return lax.dynamic_index_in_dim(x, at, 0, keepdims=False)


def per_device(tokens, teacher, left_blocks, right_blocks):
    n_z = lax.axis_size("blk")
    n_tok = lax.axis_size("tok")
    n_c = lax.axis_size(("tok", "rep"))
    z = lax.axis_index("blk")
    c = lax.axis_index(("tok", "rep"))
    plane = ("tok", "rep")
    n_b = left_blocks.shape[0]
    n_k = teacher.shape[1] // FB
    n_q = n_k // GROUP
    scale = float(tokens.shape[0] * n_c) ** (-0.5)

    left = left_blocks.reshape(n_b * BI, NB)
    rows_kb = n_k * n_b
    take = (
        lax.broadcasted_iota(jnp.int32, (rows_kb, NB), 0) // n_b + c * n_k
        == lax.broadcasted_iota(jnp.int32, (rows_kb, NB), 1)
    ).astype(BF)
    diag = (
        lax.broadcasted_iota(jnp.int32, (rows_kb, n_b * BI), 0) % n_b
        == lax.broadcasted_iota(jnp.int32, (rows_kb, n_b * BI), 1) // BI
    )
    left = lax.dot_general(take, left, NT, preferred_element_type=F32)
    left = jnp.where(diag, left, 0.0).astype(BF)

    def hidden_of(chip):
        return jnp.concatenate(
            [lax.dot_general(left, p, NT, preferred_element_type=F32).astype(BF) for p in chip], axis=1
        )

    far = [swap(tokens, "tok", s) for s in range(1, n_tok)]
    near = gather(tokens, "rep")
    first = hidden_of(near)
    early = gather(first, "blk")

    line = ("blk",) + plane
    right = right_blocks.reshape(n_q, GROUP, n_z, n_b, FB)
    bit = n_z // 2
    while bit:
        held = [a for a in range(n_z) if a % (2 * bit) == 0]
        got = lax.ppermute(right, line, [((a ^ b) * n_c + b, (a ^ b ^ bit) * n_c + b) for a in held for b in range(n_c)])
        if bit == n_z // 2:
            far, got, early[1:3] = lax.optimization_barrier((far, got, early[1:3]))
        if bit > 1:
            right = jnp.where((z ^ c) & (2 * bit - 1) == bit, got, right)
        bit //= 2

    chips = [near] + [gather(x, "rep") for x in far]
    pieces = [p for chip in chips for p in chip]
    hid = [first] + [hidden_of(chip) for chip in chips[1:]]
    late = [[swap(h, "blk", s) for s in range(1, n_z)] for h in hid[1:]]
    part, late, got = lax.optimization_barrier((target(pieces, teacher), late, got))
    right = jnp.where((z ^ c) & 1 == 1, got, right)
    resid, back = project(jnp.reshape(z, (1,)).astype(jnp.int32), part, hid, right, scale)
    order = order_of(n_z)
    backs = [back] + [swap(back[i], "blk", s) for i, s in enumerate(order) if s]
    hidden = list(zip(early, *[[h] + x for h, x in zip(hid[1:], late)]))

    mine, others = grad_right_partial([hidden[s] for s in order], resid)
    bit = 1
    while True:
        mine = mine.astype(F32) + swap(others, "blk", bit).astype(F32)
        if mine.shape[0] == 1:
            break
        mine = mine.astype(BF)
        mine, others = mine[: mine.shape[0] // 2], mine[mine.shape[0] // 2 :]
        bit *= 2
    total = lax.ppermute(
        mine[0].astype(BF), line, [(a * n_c + b, b * n_c + a) for a in range(n_z) for b in range(n_c)]
    )
    grad_right = total.reshape(n_b, n_k, FB).transpose(1, 0, 2).reshape(n_k, n_b * FB).astype(F32)

    gl = grad_left_of(backs, pieces, n_k)
    gl = gl.reshape(n_k, n_b, n_c, BI // n_c).transpose(2, 0, 3, 1).reshape(n_c, n_k, -1)
    got = []
    for s in range(n_c):
        piece = pick(gl, c ^ s)
        got.append(swap(piece, plane, s) if s else piece)
    grad_left = place(jnp.reshape(c, (1,)).astype(jnp.int32), got, n_b)

    return grad_left, grad_right


def solution(mesh):
    return jax.shard_map(
        per_device,
        mesh=mesh,
        in_specs=(
            P(("layer", "tok", "rep"), "blk"),
            P(("layer", "blk"), ("tok", "rep")),
            P(("layer", "blk"), None),
            P(("layer", "blk"), None),
        ),
        out_specs=(P(("layer", "blk"), ("tok", "rep")), P(("layer", "blk"), ("tok", "rep"))),
        check_vma=False,
    )
```

```python
import functools

import jax
import jax.numpy as jnp
from jax import lax
from jax.experimental import pallas as pl
from jax.experimental.pallas import tpu as pltpu
from jax.sharding import PartitionSpec as P

D = 8192
F = 14336
NB = 64
BI = D // NB
FB = F // NB
GROUP = 4
COLS = GROUP * FB
BF = jnp.bfloat16
F32 = jnp.float32
NT = (((1,), (1,)), ((), ()))
TN = (((0,), (0,)), ((), ()))
SPLIT = 4
VMEM = 40 * 1024 * 1024


def cost(flops, nbytes):
    return pl.CostEstimate(flops=flops, bytes_accessed=nbytes, transcendentals=0)


def rows_of(refs):
    return jnp.concatenate([r[...] for r in refs], axis=0) if len(refs) > 1 else refs[0][...]


def spread(right):
    n_z, n_k, n_b, _ = right.shape
    rows = n_z * n_k * n_b
    col = lax.broadcasted_iota(jnp.int32, (1, COLS), 1)
    tile = (lax.broadcasted_iota(jnp.int32, (FB, 1), 0) == col % FB).astype(F32).astype(BF)
    wide = jnp.dot(right.reshape(rows, FB), tile, preferred_element_type=F32)
    k_row = lax.broadcasted_iota(jnp.int32, (rows, 1), 0) // n_b % n_k
    return jnp.where(k_row == col // FB, wide, 0.0).astype(BF)


def target_kernel(pieces, *refs):
    tok_refs, teacher_refs, out_ref = refs[:pieces], refs[pieces:-1], refs[-1]
    out_ref[...] = jnp.dot(rows_of(tok_refs), rows_of(teacher_refs), preferred_element_type=F32).astype(BF)


def target(tokens, teacher):
    t, depth = tokens[0].shape
    cols = teacher.shape[1]
    block = 512 if cols % 512 == 0 else COLS
    total = t * len(tokens)
    return pl.pallas_call(
        functools.partial(target_kernel, len(tokens)),
        grid=(cols // block,),
        in_specs=[pl.BlockSpec((t, depth), lambda q: (0, 0))] * len(tokens)
        + [pl.BlockSpec((depth // SPLIT, block), lambda q, i=i: (i, q)) for i in range(SPLIT)],
        out_specs=pl.BlockSpec((total, block), lambda q: (0, q)),
        out_shape=jax.ShapeDtypeStruct((total, cols), BF),
        compiler_params=pltpu.CompilerParams(vmem_limit_bytes=VMEM),
        cost_estimate=cost(2 * total * cols * depth, 2 * depth * cols),
        name="target",
    )(*tokens, *[teacher] * SPLIT)


def project_kernel(scale, n_hid, n_z, z_ref, part_ref, *refs):
    hid_refs, right_refs, (resid_ref, back_ref) = refs[:n_hid], refs[n_hid:-2], refs[-2:]
    right = jnp.stack(
        [jnp.concatenate([a[0, :, 0], b[0, :, 0]], axis=0) for a, b in zip(right_refs[:n_z], right_refs[n_z:])],
        axis=0,
    )
    right = spread(right)
    rows = right.shape[0] // n_z
    hid = jnp.concatenate([h[...] for h in hid_refs], axis=1)
    student = lax.dot_general(hid, right[:rows], TN, preferred_element_type=F32)
    resid = ((student - part_ref[...].astype(F32)) * scale).astype(BF)
    resid_ref[...] = resid
    back = lax.dot_general(right, resid, NT, preferred_element_type=F32)
    back_ref[...] = back.astype(BF).reshape(back_ref.shape)


def project(z, part, hidden, sides, scale):
    t, cols = part.shape
    n_q, half, n_z, n_b, _ = sides[0].shape
    rows = GROUP * n_b
    right_specs = [
        pl.BlockSpec((1, half, 1, n_b, FB), lambda q, z, s=s: (q, 0, z[0] ^ s, 0, 0)) for s in range(n_z)
    ]
    return pl.pallas_call(
        functools.partial(project_kernel, scale, len(hidden), n_z),
        grid_spec=pltpu.PrefetchScalarGridSpec(
            num_scalar_prefetch=1,
            grid=(n_q,),
            in_specs=[pl.BlockSpec((t, COLS), lambda q, z: (0, q))]
            + [pl.BlockSpec((rows, h.shape[1]), lambda q, z: (q, 0)) for h in hidden]
            + right_specs * 2,
            out_specs=[
                pl.BlockSpec((t, COLS), lambda q, z: (0, q)),
                pl.BlockSpec((n_z, rows, t), lambda q, z: (0, q, 0)),
            ],
        ),
        out_shape=[
            jax.ShapeDtypeStruct((t, cols), BF),
            jax.ShapeDtypeStruct((n_z, n_q * rows, t), BF),
        ],
        compiler_params=pltpu.CompilerParams(vmem_limit_bytes=VMEM),
        cost_estimate=cost(2 * t * cols * n_z * rows * 2, 6 * t * cols),
        name="project",
    )(z, part, *hidden, *[sides[0]] * n_z, *[sides[1]] * n_z)


def grad_right_kernel(n_z, parts, *refs):
    hid_refs, (resid_ref, out_ref) = refs[:-2], refs[-2:]
    hid = jnp.concatenate(
        [
            jnp.concatenate([r[...] for r in hid_refs[s * parts : (s + 1) * parts]], axis=1)
            for s in range(n_z)
        ],
        axis=0,
    )
    prod = jnp.dot(hid, resid_ref[...], preferred_element_type=F32)
    prod = prod.reshape(n_z, GROUP, prod.shape[0] // (n_z * GROUP), COLS)
    block = lax.broadcasted_iota(jnp.int32, (1, 1, COLS), 2) // FB
    total = prod[:, 0]
    for k in range(1, GROUP):
        total = jnp.where(block == k, prod[:, k], total)
    out_ref[...] = total.astype(BF)


def grad_right_partial(hidden, resid):
    t, cols = resid.shape
    n_z, parts = len(hidden), len(hidden[0])
    n_q = cols // COLS
    rows = hidden[0][0].shape[0] // n_q
    return pl.pallas_call(
        functools.partial(grad_right_kernel, n_z, parts),
        grid=(n_q,),
        in_specs=[pl.BlockSpec((rows, h.shape[1]), lambda q: (q, 0)) for hs in hidden for h in hs]
        + [pl.BlockSpec((t, COLS), lambda q: (0, q))],
        out_specs=pl.BlockSpec((n_z, rows // GROUP, COLS), lambda q: (0, 0, q)),
        out_shape=jax.ShapeDtypeStruct((n_z, rows // GROUP, cols), BF),
        compiler_params=pltpu.CompilerParams(vmem_limit_bytes=VMEM),
        cost_estimate=cost(2 * t * cols * n_z * rows, 2 * t * cols),
        name="grad_right",
    )(*[h for hs in hidden for h in hs], resid)


def grad_left_kernel(n_z, n_k, *refs):
    back_refs, tok_refs, out_ref = refs[:n_z], refs[n_z:-1], refs[-1]
    total = back_refs[0][0].astype(F32)
    for ref in back_refs[1:]:
        total = total + ref[...].astype(F32)
    prod = jnp.dot(total.astype(BF), rows_of(tok_refs), preferred_element_type=F32)
    rows, block = prod.shape
    prod = prod.reshape(n_k, rows // n_k, block)
    at = pl.program_id(0) * (block // BI)
    own = lax.broadcasted_iota(jnp.int32, prod.shape, 1) == at + lax.broadcasted_iota(
        jnp.int32, prod.shape, 2
    ) // BI
    out_ref[...] = jnp.where(own, prod, 0.0).sum(1).astype(BF)


def grad_left_of(backs, tokens, n_k):
    n_z = len(backs)
    rows, t = backs[1].shape
    piece, depth = tokens[0].shape
    block = min(depth, 1024)
    return pl.pallas_call(
        functools.partial(grad_left_kernel, n_z, n_k),
        grid=(depth // block,),
        in_specs=[pl.BlockSpec((1, rows, t), lambda q: (0, 0, 0))]
        + [pl.BlockSpec((rows, t), lambda q: (0, 0))] * (n_z - 1)
        + [pl.BlockSpec((piece, block), lambda q: (0, q))] * len(tokens),
        out_specs=pl.BlockSpec((n_k, block), lambda q: (0, q)),
        out_shape=jax.ShapeDtypeStruct((n_k, depth), BF),
        compiler_params=pltpu.CompilerParams(vmem_limit_bytes=VMEM),
        cost_estimate=cost(2 * t * rows * depth, 2 * t * depth),
        name="grad_left",
    )(*backs, *tokens)


def place_kernel(n_b, c_ref, *refs):
    in_refs, out_ref = refs[:-1], refs[-1]
    n_c, n_k = len(in_refs), in_refs[0].shape[0]
    x = rows_of(in_refs)
    row = lax.broadcasted_iota(jnp.int32, (NB, NB), 0)
    col = lax.broadcasted_iota(jnp.int32, (NB, NB), 1)
    pick = row == ((col // n_k) ^ c_ref[0]) * n_k + col % n_k
    got = lax.dot_general(
        x, pick.astype(F32).astype(BF), (((0,), (1,)), ((), ())), preferred_element_type=F32
    )
    for j in range(got.shape[0] // n_b):
        out_ref[:, j * NB : (j + 1) * NB] = got[j * n_b : (j + 1) * n_b]


def place(c, pieces, n_b):
    n = pieces[0].shape[1] // n_b
    return pl.pallas_call(
        functools.partial(place_kernel, n_b),
        in_specs=[pl.BlockSpec(memory_space=pltpu.SMEM)]
        + [pl.BlockSpec(memory_space=pltpu.VMEM)] * len(pieces),
        out_specs=pl.BlockSpec(memory_space=pltpu.VMEM),
        out_shape=jax.ShapeDtypeStruct((n_b, n * NB), F32),
        name="place",
    )(c, *pieces)


def swap(x, axes, s):
    n = lax.axis_size(axes)
    return lax.ppermute(x, axes, [(i, i ^ s) for i in range(n)])


def gather(x, axes):
    got = [x]
    for s in range(1, lax.axis_size(axes)):
        got.append(swap(got[s & (s - 1)], axes, s & -s))
    return got


def pick(x, at):
    return lax.dynamic_index_in_dim(x, at, 0, keepdims=False)


def per_device(tokens, teacher, left_blocks, right_blocks):
    n_z = lax.axis_size("blk")
    n_tok = lax.axis_size("tok")
    n_c = lax.axis_size(("tok", "rep"))
    z = lax.axis_index("blk")
    c = lax.axis_index(("tok", "rep"))
    plane = ("tok", "rep")
    n_b = left_blocks.shape[0]
    n_k = teacher.shape[1] // FB
    n_q = n_k // GROUP
    scale = float(tokens.shape[0] * n_c) ** (-0.5)

    left = left_blocks.reshape(n_b * BI, NB)
    rows_kb = n_k * n_b
    take = (
        lax.broadcasted_iota(jnp.int32, (rows_kb, NB), 0) // n_b + c * n_k
        == lax.broadcasted_iota(jnp.int32, (rows_kb, NB), 1)
    ).astype(BF)
    diag = (
        lax.broadcasted_iota(jnp.int32, (rows_kb, n_b * BI), 0) % n_b
        == lax.broadcasted_iota(jnp.int32, (rows_kb, n_b * BI), 1) // BI
    )
    left = lax.dot_general(take, left, NT, preferred_element_type=F32)
    left = jnp.where(diag, left, 0.0).astype(BF)

    def hidden_of(chip):
        return jnp.concatenate(
            [lax.dot_general(left, p, NT, preferred_element_type=F32).astype(BF) for p in chip], axis=1
        )

    far = [swap(tokens, "tok", s) for s in range(1, n_tok)]
    near = gather(tokens, "rep")
    first = hidden_of(near)

    sides = right_blocks.reshape(n_q, 2, GROUP // 2, n_z, n_b, FB)
    sides = [sides[:, i] for i in range(2)]
    far, first = lax.optimization_barrier((far, first))
    turn = [
        [(a * n_c + b, (b ^ side) * n_c + a) for a in range(n_z) for b in range(n_c)] for side in (0, n_c // 2)
    ]
    sides = [lax.ppermute(x, ("blk",) + plane, perm) for x, perm in zip(sides, turn)]

    chips = [near] + [gather(x, "rep") for x in far]
    pieces = [p for chip in chips for p in chip]
    hid = [jnp.concatenate([first] + [hidden_of(chip) for chip in chips[1:]], axis=1)]
    hidden = hid + [swap(hid[0], "blk", s) for s in (1, 2)]
    part, hidden[1:], sides = lax.optimization_barrier((target(pieces, teacher), hidden[1:], sides))
    for s in range(3, n_z):
        hidden.append(swap(hidden[s & (s - 1)], "blk", s & -s))
    hidden = [[h] for h in hidden]
    resid, back = project(jnp.reshape(z, (1,)).astype(jnp.int32), part, hid, sides, scale)
    backs = [back] + [swap(back[s], "blk", s) for s in range(1, n_z)]

    gr = grad_right_partial(hidden, resid)
    total = gr[0].astype(F32)
    for s in range(1, n_z):
        total = total + swap(gr[s], "blk", s).astype(F32)
    total = lax.ppermute(total.astype(BF), ("blk",) + plane, turn[0])
    grad_right = total.reshape(n_b, n_k, FB).transpose(1, 0, 2).reshape(n_k, n_b * FB).astype(F32)

    gl = grad_left_of(backs, pieces, n_k)
    gl = gl.reshape(n_k, n_b, n_c, BI // n_c).transpose(2, 0, 3, 1).reshape(n_c, n_k, -1)
    got = []
    for s in range(n_c):
        piece = pick(gl, c ^ s)
        got.append(swap(piece, plane, s) if s else piece)
    grad_left = place(jnp.reshape(c, (1,)).astype(jnp.int32), got, n_b)

    return grad_left, grad_right


def solution(mesh):
    return jax.shard_map(
        per_device,
        mesh=mesh,
        in_specs=(
            P(("layer", "tok", "rep"), "blk"),
            P(("layer", "blk"), ("tok", "rep")),
            P(("layer", "blk"), None),
            P(("layer", "blk"), None),
        ),
        out_specs=(P(("layer", "blk"), ("tok", "rep")), P(("layer", "blk"), ("tok", "rep"))),
        check_vma=False,
    )
```

```python
import functools

import jax
import jax.numpy as jnp
from jax import lax
from jax.experimental import pallas as pl
from jax.experimental.pallas import tpu as pltpu
from jax.sharding import PartitionSpec as P

D = 8192
F = 14336
NB = 64
BI = D // NB
FB = F // NB
GROUP = 4
COLS = GROUP * FB
BF = jnp.bfloat16
F32 = jnp.float32
NT = (((1,), (1,)), ((), ()))
TN = (((0,), (0,)), ((), ()))
SPLIT = 4
VMEM = 40 * 1024 * 1024


def cost(flops, nbytes):
    return pl.CostEstimate(flops=flops, bytes_accessed=nbytes, transcendentals=0)


def rows_of(refs):
    return jnp.concatenate([r[...] for r in refs], axis=0) if len(refs) > 1 else refs[0][...]


def spread(right):
    n_z, n_k, n_b, _ = right.shape
    rows = n_z * n_k * n_b
    col = lax.broadcasted_iota(jnp.int32, (1, COLS), 1)
    tile = (lax.broadcasted_iota(jnp.int32, (FB, 1), 0) == col % FB).astype(F32).astype(BF)
    wide = jnp.dot(right.reshape(rows, FB), tile, preferred_element_type=F32)
    k_row = lax.broadcasted_iota(jnp.int32, (rows, 1), 0) // n_b % n_k
    return jnp.where(k_row == col // FB, wide, 0.0).astype(BF)


def target_kernel(pieces, *refs):
    tok_refs, teacher_refs, out_ref = refs[:pieces], refs[pieces:-1], refs[-1]
    out_ref[...] = jnp.dot(rows_of(tok_refs), rows_of(teacher_refs), preferred_element_type=F32).astype(BF)


def target(tokens, teacher):
    t, depth = tokens[0].shape
    cols = teacher.shape[1]
    block = 512 if cols % 512 == 0 else COLS
    total = t * len(tokens)
    return pl.pallas_call(
        functools.partial(target_kernel, len(tokens)),
        grid=(cols // block,),
        in_specs=[pl.BlockSpec((t, depth), lambda q: (0, 0))] * len(tokens)
        + [pl.BlockSpec((depth // SPLIT, block), lambda q, i=i: (i, q)) for i in range(SPLIT)],
        out_specs=pl.BlockSpec((total, block), lambda q: (0, q)),
        out_shape=jax.ShapeDtypeStruct((total, cols), BF),
        compiler_params=pltpu.CompilerParams(vmem_limit_bytes=VMEM),
        cost_estimate=cost(2 * total * cols * depth, 2 * depth * cols),
        name="target",
    )(*tokens, *[teacher] * SPLIT)


def project_kernel(scale, n_hid, n_z, z_ref, part_ref, *refs):
    hid_refs, right_refs, (resid_ref, back_ref) = refs[:n_hid], refs[n_hid:-2], refs[-2:]
    right = jnp.stack(
        [jnp.concatenate([a[0, :, 0], b[0, :, 0]], axis=0) for a, b in zip(right_refs[:n_z], right_refs[n_z:])],
        axis=0,
    )
    right = spread(right)
    rows = right.shape[0] // n_z
    hid = jnp.concatenate([h[...] for h in hid_refs], axis=1)
    student = lax.dot_general(hid, right[:rows], TN, preferred_element_type=F32)
    resid = ((student - part_ref[...].astype(F32)) * scale).astype(BF)
    resid_ref[...] = resid
    back = lax.dot_general(right, resid, NT, preferred_element_type=F32)
    back_ref[...] = back.astype(BF).reshape(back_ref.shape)


def project(z, part, hidden, sides, scale):
    t, cols = part.shape
    n_q, half, n_z, n_b, _ = sides[0].shape
    rows = GROUP * n_b
    right_specs = [
        pl.BlockSpec((1, half, 1, n_b, FB), lambda q, z, s=s: (q, 0, z[0] ^ s, 0, 0)) for s in range(n_z)
    ]
    return pl.pallas_call(
        functools.partial(project_kernel, scale, len(hidden), n_z),
        grid_spec=pltpu.PrefetchScalarGridSpec(
            num_scalar_prefetch=1,
            grid=(n_q,),
            in_specs=[pl.BlockSpec((t, COLS), lambda q, z: (0, q))]
            + [pl.BlockSpec((rows, h.shape[1]), lambda q, z: (q, 0)) for h in hidden]
            + right_specs * 2,
            out_specs=[
                pl.BlockSpec((t, COLS), lambda q, z: (0, q)),
                pl.BlockSpec((n_z, rows, t), lambda q, z: (0, q, 0)),
            ],
        ),
        out_shape=[
            jax.ShapeDtypeStruct((t, cols), BF),
            jax.ShapeDtypeStruct((n_z, n_q * rows, t), BF),
        ],
        compiler_params=pltpu.CompilerParams(vmem_limit_bytes=VMEM),
        cost_estimate=cost(2 * t * cols * n_z * rows * 2, 6 * t * cols),
        name="project",
    )(z, part, *hidden, *[sides[0]] * n_z, *[sides[1]] * n_z)


def grad_right_kernel(n_z, parts, *refs):
    hid_refs, (resid_ref, out_ref) = refs[:-2], refs[-2:]
    hid = jnp.concatenate(
        [
            jnp.concatenate([r[...] for r in hid_refs[s * parts : (s + 1) * parts]], axis=1)
            for s in range(n_z)
        ],
        axis=0,
    )
    prod = jnp.dot(hid, resid_ref[...], preferred_element_type=F32)
    prod = prod.reshape(n_z, GROUP, prod.shape[0] // (n_z * GROUP), COLS)
    block = lax.broadcasted_iota(jnp.int32, (1, 1, COLS), 2) // FB
    total = prod[:, 0]
    for k in range(1, GROUP):
        total = jnp.where(block == k, prod[:, k], total)
    out_ref[...] = total.astype(BF)


def grad_right_partial(hidden, resid):
    t, cols = resid.shape
    n_z, parts = len(hidden), len(hidden[0])
    n_q = cols // COLS
    rows = hidden[0][0].shape[0] // n_q
    return pl.pallas_call(
        functools.partial(grad_right_kernel, n_z, parts),
        grid=(n_q,),
        in_specs=[pl.BlockSpec((rows, h.shape[1]), lambda q: (q, 0)) for hs in hidden for h in hs]
        + [pl.BlockSpec((t, COLS), lambda q: (0, q))],
        out_specs=pl.BlockSpec((n_z, rows // GROUP, COLS), lambda q: (0, 0, q)),
        out_shape=jax.ShapeDtypeStruct((n_z, rows // GROUP, cols), BF),
        compiler_params=pltpu.CompilerParams(vmem_limit_bytes=VMEM),
        cost_estimate=cost(2 * t * cols * n_z * rows, 2 * t * cols),
        name="grad_right",
    )(*[h for hs in hidden for h in hs], resid)


def grad_left_kernel(n_z, n_k, *refs):
    back_refs, tok_refs, out_ref = refs[:n_z], refs[n_z:-1], refs[-1]
    total = back_refs[0][0].astype(F32)
    for ref in back_refs[1:]:
        total = total + ref[...].astype(F32)
    prod = jnp.dot(total.astype(BF), rows_of(tok_refs), preferred_element_type=F32)
    rows, block = prod.shape
    prod = prod.reshape(n_k, rows // n_k, block)
    at = pl.program_id(0) * (block // BI)
    own = lax.broadcasted_iota(jnp.int32, prod.shape, 1) == at + lax.broadcasted_iota(
        jnp.int32, prod.shape, 2
    ) // BI
    out_ref[...] = jnp.where(own, prod, 0.0).sum(1).astype(BF)


def grad_left_of(backs, tokens, n_k):
    n_z = len(backs)
    rows, t = backs[1].shape
    piece, depth = tokens[0].shape
    block = min(depth, 1024)
    return pl.pallas_call(
        functools.partial(grad_left_kernel, n_z, n_k),
        grid=(depth // block,),
        in_specs=[pl.BlockSpec((1, rows, t), lambda q: (0, 0, 0))]
        + [pl.BlockSpec((rows, t), lambda q: (0, 0))] * (n_z - 1)
        + [pl.BlockSpec((piece, block), lambda q: (0, q))] * len(tokens),
        out_specs=pl.BlockSpec((n_k, block), lambda q: (0, q)),
        out_shape=jax.ShapeDtypeStruct((n_k, depth), BF),
        compiler_params=pltpu.CompilerParams(vmem_limit_bytes=VMEM),
        cost_estimate=cost(2 * t * rows * depth, 2 * t * depth),
        name="grad_left",
    )(*backs, *tokens)


def place_kernel(n_b, c_ref, *refs):
    in_refs, out_ref = refs[:-1], refs[-1]
    n_c, n_k = len(in_refs), in_refs[0].shape[0]
    x = rows_of(in_refs)
    row = lax.broadcasted_iota(jnp.int32, (NB, NB), 0)
    col = lax.broadcasted_iota(jnp.int32, (NB, NB), 1)
    pick = row == ((col // n_k) ^ c_ref[0]) * n_k + col % n_k
    got = lax.dot_general(
        x, pick.astype(F32).astype(BF), (((0,), (1,)), ((), ())), preferred_element_type=F32
    )
    for j in range(got.shape[0] // n_b):
        out_ref[:, j * NB : (j + 1) * NB] = got[j * n_b : (j + 1) * n_b]


def place(c, pieces, n_b):
    n = pieces[0].shape[1] // n_b
    return pl.pallas_call(
        functools.partial(place_kernel, n_b),
        in_specs=[pl.BlockSpec(memory_space=pltpu.SMEM)]
        + [pl.BlockSpec(memory_space=pltpu.VMEM)] * len(pieces),
        out_specs=pl.BlockSpec(memory_space=pltpu.VMEM),
        out_shape=jax.ShapeDtypeStruct((n_b, n * NB), F32),
        name="place",
    )(c, *pieces)


def swap(x, axes, s):
    n = lax.axis_size(axes)
    return lax.ppermute(x, axes, [(i, i ^ s) for i in range(n)])


def gather(x, axes):
    got = [x]
    for s in range(1, lax.axis_size(axes)):
        got.append(swap(got[s & (s - 1)], axes, s & -s))
    return got


def pick(x, at):
    return lax.dynamic_index_in_dim(x, at, 0, keepdims=False)


def per_device(tokens, teacher, left_blocks, right_blocks):
    n_z = lax.axis_size("blk")
    n_tok = lax.axis_size("tok")
    n_c = lax.axis_size(("tok", "rep"))
    z = lax.axis_index("blk")
    c = lax.axis_index(("tok", "rep"))
    plane = ("tok", "rep")
    n_b = left_blocks.shape[0]
    n_k = teacher.shape[1] // FB
    n_q = n_k // GROUP
    scale = float(tokens.shape[0] * n_c) ** (-0.5)

    left = left_blocks.reshape(n_b * BI, NB)
    rows_kb = n_k * n_b
    take = (
        lax.broadcasted_iota(jnp.int32, (rows_kb, NB), 0) // n_b + c * n_k
        == lax.broadcasted_iota(jnp.int32, (rows_kb, NB), 1)
    ).astype(BF)
    diag = (
        lax.broadcasted_iota(jnp.int32, (rows_kb, n_b * BI), 0) % n_b
        == lax.broadcasted_iota(jnp.int32, (rows_kb, n_b * BI), 1) // BI
    )
    left = lax.dot_general(take, left, NT, preferred_element_type=F32)
    left = jnp.where(diag, left, 0.0).astype(BF)

    def hidden_of(chip):
        return jnp.concatenate(
            [lax.dot_general(left, p, NT, preferred_element_type=F32).astype(BF) for p in chip], axis=1
        )

    far = [swap(tokens, "tok", s) for s in range(1, n_tok)]
    near = gather(tokens, "rep")
    first = hidden_of(near)

    sides = right_blocks.reshape(n_q, 2, GROUP // 2, n_z, n_b, FB)
    turn = [
        [(a * n_c + b, (b ^ side) * n_c + a) for a in range(n_z) for b in range(n_c)] for side in (0, n_c // 2)
    ]
    sides = [lax.ppermute(sides[:, i], ("blk",) + plane, perm) for i, perm in enumerate(turn)]
    far, first, sides = lax.optimization_barrier((far, first, sides))

    chips = [near] + [gather(x, "rep") for x in far]
    pieces = [p for chip in chips for p in chip]
    hid = [jnp.concatenate([first] + [hidden_of(chip) for chip in chips[1:]], axis=1)]
    hidden = hid + [swap(hid[0], "blk", s) for s in (1, 2)]
    part, hidden[1:] = lax.optimization_barrier((target(pieces, teacher), hidden[1:]))
    for s in range(3, n_z):
        hidden.append(swap(hidden[s & (s - 1)], "blk", s & -s))
    hidden = [[h] for h in hidden]
    resid, back = project(jnp.reshape(z, (1,)).astype(jnp.int32), part, hid, sides, scale)
    backs = [back] + [swap(back[s], "blk", s) for s in range(1, n_z)]

    gr = grad_right_partial(hidden, resid)
    there = []
    for s in range(n_c):
        piece = pick(gr, z ^ c ^ s)
        there.append(swap(piece, plane, s) if s else piece)
    there = jnp.stack(there, 0)
    total = None
    for s in range(n_z):
        piece = pick(there, c ^ z ^ s)
        piece = (swap(piece, "blk", s) if s else piece).astype(F32)
        total = piece if total is None else total + piece
    grad_right = total.reshape(n_b, n_k, FB).transpose(1, 0, 2).reshape(n_k, n_b * FB)

    gl = grad_left_of(backs, pieces, n_k)
    gl = gl.reshape(n_k, n_b, n_c, BI // n_c).transpose(2, 0, 3, 1).reshape(n_c, n_k, -1)
    got = []
    for s in range(n_c):
        piece = pick(gl, c ^ s)
        got.append(swap(piece, plane, s) if s else piece)
    grad_left = place(jnp.reshape(c, (1,)).astype(jnp.int32), got, n_b)

    return grad_left, grad_right


def solution(mesh):
    return jax.shard_map(
        per_device,
        mesh=mesh,
        in_specs=(
            P(("layer", "tok", "rep"), "blk"),
            P(("layer", "blk"), ("tok", "rep")),
            P(("layer", "blk"), None),
            P(("layer", "blk"), None),
        ),
        out_specs=(P(("layer", "blk"), ("tok", "rep")), P(("layer", "blk"), ("tok", "rep"))),
        check_vma=False,
    )
```

```python
import functools

import jax
import jax.numpy as jnp
from jax import lax
from jax.experimental import pallas as pl
from jax.experimental.pallas import tpu as pltpu
from jax.sharding import PartitionSpec as P

D = 8192
F = 14336
NB = 64
BI = D // NB
FB = F // NB
GROUP = 4
COLS = GROUP * FB
BF = jnp.bfloat16
F32 = jnp.float32
NT = (((1,), (1,)), ((), ()))
TN = (((0,), (0,)), ((), ()))
SPLIT = 4
VMEM = 40 * 1024 * 1024


def cost(flops, nbytes):
    return pl.CostEstimate(flops=flops, bytes_accessed=nbytes, transcendentals=0)


def rows_of(refs):
    return jnp.concatenate([r[...] for r in refs], axis=0) if len(refs) > 1 else refs[0][...]


def spread(right):
    n_z, n_k, n_b, _ = right.shape
    rows = n_z * n_k * n_b
    col = lax.broadcasted_iota(jnp.int32, (1, COLS), 1)
    tile = (lax.broadcasted_iota(jnp.int32, (FB, 1), 0) == col % FB).astype(F32).astype(BF)
    wide = jnp.dot(right.reshape(rows, FB), tile, preferred_element_type=F32)
    k_row = lax.broadcasted_iota(jnp.int32, (rows, 1), 0) // n_b % n_k
    return jnp.where(k_row == col // FB, wide, 0.0).astype(BF)


def target_kernel(pieces, *refs):
    tok_refs, teacher_refs, out_ref = refs[:pieces], refs[pieces:-1], refs[-1]
    out_ref[...] = jnp.dot(rows_of(tok_refs), rows_of(teacher_refs), preferred_element_type=F32).astype(BF)


def target(tokens, teacher):
    t, depth = tokens[0].shape
    cols = teacher.shape[1]
    block = 512 if cols % 512 == 0 else COLS
    total = t * len(tokens)
    return pl.pallas_call(
        functools.partial(target_kernel, len(tokens)),
        grid=(cols // block,),
        in_specs=[pl.BlockSpec((t, depth), lambda q: (0, 0))] * len(tokens)
        + [pl.BlockSpec((depth // SPLIT, block), lambda q, i=i: (i, q)) for i in range(SPLIT)],
        out_specs=pl.BlockSpec((total, block), lambda q: (0, q)),
        out_shape=jax.ShapeDtypeStruct((total, cols), BF),
        compiler_params=pltpu.CompilerParams(vmem_limit_bytes=VMEM),
        cost_estimate=cost(2 * total * cols * depth, 2 * depth * cols),
        name="target",
    )(*tokens, *[teacher] * SPLIT)


def project_kernel(scale, n_hid, n_z, z_ref, part_ref, *refs):
    hid_refs, right_refs, refs = refs[:n_hid], refs[n_hid : n_hid + 2 * n_z], refs[n_hid + 2 * n_z :]
    resid_ref, *back_refs = refs
    right = jnp.stack(
        [jnp.concatenate([a[0, :, 0], b[0, :, 0]], axis=0) for a, b in zip(right_refs[:n_z], right_refs[n_z:])],
        axis=0,
    )
    right = spread(right)
    rows = right.shape[0] // n_z
    hid = jnp.concatenate([h[...] for h in hid_refs], axis=1)
    student = lax.dot_general(hid, right[:rows], TN, preferred_element_type=F32)
    resid = ((student - part_ref[...].astype(F32)) * scale).astype(BF)
    resid_ref[...] = resid
    back = lax.dot_general(right, resid, NT, preferred_element_type=F32)
    for s, ref in enumerate(back_refs):
        ref[...] = back[s * rows : (s + 1) * rows].astype(BF)


def project(z, part, hidden, sides, scale):
    t, cols = part.shape
    n_q, half, n_z, n_b, _ = sides[0].shape
    rows = GROUP * n_b
    right_specs = [
        pl.BlockSpec((1, half, 1, n_b, FB), lambda q, z, s=s: (q, 0, z[0] ^ s, 0, 0)) for s in range(n_z)
    ]
    return pl.pallas_call(
        functools.partial(project_kernel, scale, len(hidden), n_z),
        grid_spec=pltpu.PrefetchScalarGridSpec(
            num_scalar_prefetch=1,
            grid=(n_q,),
            in_specs=[pl.BlockSpec((t, COLS), lambda q, z: (0, q))]
            + [pl.BlockSpec((rows, h.shape[1]), lambda q, z: (q, 0)) for h in hidden]
            + right_specs * 2,
            out_specs=[pl.BlockSpec((t, COLS), lambda q, z: (0, q))]
            + [pl.BlockSpec((rows, t), lambda q, z: (q, 0))] * n_z,
        ),
        out_shape=[jax.ShapeDtypeStruct((t, cols), BF)]
        + [jax.ShapeDtypeStruct((n_q * rows, t), BF)] * n_z,
        compiler_params=pltpu.CompilerParams(vmem_limit_bytes=VMEM),
        cost_estimate=cost(2 * t * cols * n_z * rows * 2, 6 * t * cols),
        name="project",
    )(z, part, *hidden, *[sides[0]] * n_z, *[sides[1]] * n_z)


def grad_right_kernel(*refs):
    *hid_refs, resid_ref, out_ref = refs
    n_z, rows = len(hid_refs), hid_refs[0].shape[1]
    hid = jnp.concatenate([r[0] for r in hid_refs], axis=0)
    prod = jnp.dot(hid, resid_ref[...], preferred_element_type=F32)
    prod = prod.reshape(n_z, GROUP, rows // GROUP, COLS)
    block = lax.broadcasted_iota(jnp.int32, (1, 1, COLS), 2) // FB
    total = prod[:, 0]
    for k in range(1, GROUP):
        total = jnp.where(block == k, prod[:, k], total)
    out_ref[...] = total.astype(BF)


def grad_right_partial(hidden, resid):
    t, cols = resid.shape
    n_z, n_q = len(hidden), cols // COLS
    rows = hidden[0][0].shape[1] // n_q
    return pl.pallas_call(
        grad_right_kernel,
        grid=(n_q,),
        in_specs=[pl.BlockSpec((1, rows, t), lambda q, i=i: (i, q, 0)) for _, i in hidden]
        + [pl.BlockSpec((t, COLS), lambda q: (0, q))],
        out_specs=pl.BlockSpec((n_z, rows // GROUP, COLS), lambda q: (0, 0, q)),
        out_shape=jax.ShapeDtypeStruct((n_z, rows // GROUP, cols), BF),
        compiler_params=pltpu.CompilerParams(vmem_limit_bytes=VMEM),
        cost_estimate=cost(2 * t * cols * n_z * rows, 2 * t * cols),
        name="grad_right",
    )(*[h for h, _ in hidden], resid)


def grad_left_kernel(n_z, n_k, *refs):
    back_refs, tok_refs, out_ref = refs[:n_z], refs[n_z:-1], refs[-1]
    total = back_refs[0][...].astype(F32)
    for ref in back_refs[1:]:
        total = total + ref[...].astype(F32)
    prod = jnp.dot(total.astype(BF), rows_of(tok_refs), preferred_element_type=F32)
    rows, block = prod.shape
    prod = prod.reshape(n_k, rows // n_k, block)
    at = pl.program_id(0) * (block // BI)
    own = lax.broadcasted_iota(jnp.int32, prod.shape, 1) == at + lax.broadcasted_iota(
        jnp.int32, prod.shape, 2
    ) // BI
    out_ref[...] = jnp.where(own, prod, 0.0).sum(1).astype(BF)


def grad_left_of(backs, tokens, n_k):
    n_z = len(backs)
    rows, t = backs[1].shape
    piece, depth = tokens[0].shape
    block = min(depth, 1024)
    return pl.pallas_call(
        functools.partial(grad_left_kernel, n_z, n_k),
        grid=(depth // block,),
        in_specs=[pl.BlockSpec((rows, t), lambda q: (0, 0))] * n_z
        + [pl.BlockSpec((piece, block), lambda q: (0, q))] * len(tokens),
        out_specs=pl.BlockSpec((n_k, block), lambda q: (0, q)),
        out_shape=jax.ShapeDtypeStruct((n_k, depth), BF),
        compiler_params=pltpu.CompilerParams(vmem_limit_bytes=VMEM),
        cost_estimate=cost(2 * t * rows * depth, 2 * t * depth),
        name="grad_left",
    )(*backs, *tokens)


def place_kernel(n_b, c_ref, *refs):
    in_refs, out_ref = refs[:-1], refs[-1]
    n_c, n_k = len(in_refs), in_refs[0].shape[0]
    x = rows_of(in_refs)
    row = lax.broadcasted_iota(jnp.int32, (NB, NB), 0)
    col = lax.broadcasted_iota(jnp.int32, (NB, NB), 1)
    pick = row == ((col // n_k) ^ c_ref[0]) * n_k + col % n_k
    got = lax.dot_general(
        x, pick.astype(F32).astype(BF), (((0,), (1,)), ((), ())), preferred_element_type=F32
    )
    for j in range(got.shape[0] // n_b):
        out_ref[:, j * NB : (j + 1) * NB] = got[j * n_b : (j + 1) * n_b]


def place(c, pieces, n_b):
    n = pieces[0].shape[1] // n_b
    return pl.pallas_call(
        functools.partial(place_kernel, n_b),
        in_specs=[pl.BlockSpec(memory_space=pltpu.SMEM)]
        + [pl.BlockSpec(memory_space=pltpu.VMEM)] * len(pieces),
        out_specs=pl.BlockSpec(memory_space=pltpu.VMEM),
        out_shape=jax.ShapeDtypeStruct((n_b, n * NB), F32),
        name="place",
    )(c, *pieces)


def swap(x, axes, s):
    n = lax.axis_size(axes)
    return lax.ppermute(x, axes, [(i, i ^ s) for i in range(n)])


def gather(x, axes):
    got = [x]
    for s in range(1, lax.axis_size(axes)):
        got.append(swap(got[s & (s - 1)], axes, s & -s))
    return got


def pick(x, at):
    return lax.dynamic_index_in_dim(x, at, 0, keepdims=False)


def per_device(tokens, teacher, left_blocks, right_blocks):
    n_z = lax.axis_size("blk")
    n_tok = lax.axis_size("tok")
    n_c = lax.axis_size(("tok", "rep"))
    z = lax.axis_index("blk")
    c = lax.axis_index(("tok", "rep"))
    plane = ("tok", "rep")
    n_b = left_blocks.shape[0]
    n_k = teacher.shape[1] // FB
    n_q = n_k // GROUP
    scale = float(tokens.shape[0] * n_c) ** (-0.5)

    left = left_blocks.reshape(n_b * BI, NB)
    rows_kb = n_k * n_b
    take = (
        lax.broadcasted_iota(jnp.int32, (rows_kb, NB), 0) // n_b + c * n_k
        == lax.broadcasted_iota(jnp.int32, (rows_kb, NB), 1)
    ).astype(BF)
    diag = (
        lax.broadcasted_iota(jnp.int32, (rows_kb, n_b * BI), 0) % n_b
        == lax.broadcasted_iota(jnp.int32, (rows_kb, n_b * BI), 1) // BI
    )
    left = lax.dot_general(take, left, NT, preferred_element_type=F32)
    left = jnp.where(diag, left, 0.0).astype(BF)

    def hidden_of(chip):
        return jnp.concatenate(
            [lax.dot_general(left, p, NT, preferred_element_type=F32).astype(BF) for p in chip], axis=1
        )

    far = [swap(tokens, "tok", s) for s in range(1, n_tok)]
    near = gather(tokens, "rep")
    first = hidden_of(near)

    sides = right_blocks.reshape(n_q, 2, GROUP // 2, n_z, n_b, FB)
    turn = [
        [(a * n_c + b, (b ^ side) * n_c + a) for a in range(n_z) for b in range(n_c)] for side in (0, n_c // 2)
    ]
    sides = [lax.ppermute(sides[:, i], ("blk",) + plane, perm) for i, perm in enumerate(turn)]
    far, first, sides = lax.optimization_barrier((far, first, sides))

    chips = [near] + [gather(x, "rep") for x in far]
    pieces = [p for chip in chips for p in chip]
    hid = [jnp.concatenate([first] + [hidden_of(chip) for chip in chips[1:]], axis=1)]
    bit = n_z // 2
    got = swap(hid[0], "blk", bit)
    part, got = lax.optimization_barrier((target(pieces, teacher), got))
    hidden, order, got = [hid[0][None]], [0], got[None]
    while True:
        hidden.append(got)
        order += [o ^ bit for o in order]
        bit //= 2
        if bit == 0:
            break
        got = swap(jnp.concatenate(hidden, axis=0), "blk", bit)
    where = [(x, i) for x in hidden for i in range(x.shape[0])]
    hidden = [where[order.index(s)] for s in range(n_z)]
    resid, *back = project(jnp.reshape(z, (1,)).astype(jnp.int32), part, hid, sides, scale)
    backs = back[:1] + [swap(back[s], "blk", s) for s in range(1, n_z)]

    gr = grad_right_partial(hidden, resid)
    there = []
    for s in range(n_c):
        piece = pick(gr, z ^ c ^ s)
        there.append(swap(piece, plane, s) if s else piece)
    there = jnp.stack(there, 0)
    total = None
    for s in range(n_z):
        piece = pick(there, c ^ z ^ s)
        piece = (swap(piece, "blk", s) if s else piece).astype(F32)
        total = piece if total is None else total + piece
    grad_right = total.reshape(n_b, n_k, FB).transpose(1, 0, 2).reshape(n_k, n_b * FB)

    gl = grad_left_of(backs, pieces, n_k)
    gl = gl.reshape(n_k, n_b, n_c, BI // n_c).transpose(2, 0, 3, 1).reshape(n_c, n_k, -1)
    got = []
    for s in range(n_c):
        piece = pick(gl, c ^ s)
        got.append(swap(piece, plane, s) if s else piece)
    grad_left = place(jnp.reshape(c, (1,)).astype(jnp.int32), got, n_b)

    return grad_left, grad_right


def solution(mesh):
    return jax.shard_map(
        per_device,
        mesh=mesh,
        in_specs=(
            P(("layer", "tok", "rep"), "blk"),
            P(("layer", "blk"), ("tok", "rep")),
            P(("layer", "blk"), None),
            P(("layer", "blk"), None),
        ),
        out_specs=(P(("layer", "blk"), ("tok", "rep")), P(("layer", "blk"), ("tok", "rep"))),
        check_vma=False,
    )
```

```python
import functools

import jax
import jax.numpy as jnp
from jax import lax
from jax.experimental import pallas as pl
from jax.experimental.pallas import tpu as pltpu
from jax.sharding import PartitionSpec as P

D = 8192
F = 14336
NB = 64
BI = D // NB
FB = F // NB
GROUP = 4
COLS = GROUP * FB
BF = jnp.bfloat16
F32 = jnp.float32
NT = (((1,), (1,)), ((), ()))
TN = (((0,), (0,)), ((), ()))
SPLIT = 4
VMEM = 20 * 1024 * 1024


def cost(flops, nbytes):
    return pl.CostEstimate(flops=flops, bytes_accessed=nbytes, transcendentals=0)


def rows_of(refs):
    return jnp.concatenate([r[...] for r in refs], axis=0) if len(refs) > 1 else refs[0][...]


def spread(right):
    n_z, n_k, n_b, _ = right.shape
    rows = n_z * n_k * n_b
    col = lax.broadcasted_iota(jnp.int32, (1, COLS), 1)
    tile = (lax.broadcasted_iota(jnp.int32, (FB, 1), 0) == col % FB).astype(F32).astype(BF)
    wide = jnp.dot(right.reshape(rows, FB), tile, preferred_element_type=F32)
    k_row = lax.broadcasted_iota(jnp.int32, (rows, 1), 0) // n_b % n_k
    return jnp.where(k_row == col // FB, wide, 0.0).astype(BF)


def target_kernel(pieces, *refs):
    tok_refs, teacher_refs, out_ref = refs[:pieces], refs[pieces:-1], refs[-1]
    out_ref[...] = jnp.dot(rows_of(tok_refs), rows_of(teacher_refs), preferred_element_type=F32).astype(BF)


def target(tokens, teacher):
    t, depth = tokens[0].shape
    cols = teacher.shape[1]
    block = 512 if cols % 512 == 0 else COLS
    total = t * len(tokens)
    return pl.pallas_call(
        functools.partial(target_kernel, len(tokens)),
        grid=(cols // block,),
        in_specs=[pl.BlockSpec((t, depth), lambda q: (0, 0))] * len(tokens)
        + [pl.BlockSpec((depth // SPLIT, block), lambda q, i=i: (i, q)) for i in range(SPLIT)],
        out_specs=pl.BlockSpec((total, block), lambda q: (0, q)),
        out_shape=jax.ShapeDtypeStruct((total, cols), BF),
        compiler_params=pltpu.CompilerParams(vmem_limit_bytes=VMEM),
        cost_estimate=cost(2 * total * cols * depth, 2 * depth * cols),
        name="target",
    )(*tokens, *[teacher] * SPLIT)


def project_kernel(scale, n_hid, n_z, z_ref, part_ref, *refs):
    hid_refs, right_refs, refs = refs[:n_hid], refs[n_hid : n_hid + 2 * n_z], refs[n_hid + 2 * n_z :]
    resid_ref, *back_refs = refs
    right = jnp.stack(
        [jnp.concatenate([a[0, :, 0], b[0, :, 0]], axis=0) for a, b in zip(right_refs[:n_z], right_refs[n_z:])],
        axis=0,
    )
    right = spread(right)
    rows = right.shape[0] // n_z
    hid = jnp.concatenate([h[...] for h in hid_refs], axis=1)
    student = lax.dot_general(hid, right[:rows], TN, preferred_element_type=F32)
    resid = ((student - part_ref[...].astype(F32)) * scale).astype(BF)
    resid_ref[...] = resid
    back = lax.dot_general(right, resid, NT, preferred_element_type=F32)
    for s, ref in enumerate(back_refs):
        ref[...] = back[s * rows : (s + 1) * rows].astype(BF)


def project(z, part, hidden, sides, scale):
    t, cols = part.shape
    n_q, half, n_z, n_b, _ = sides[0].shape
    rows = GROUP * n_b
    right_specs = [
        pl.BlockSpec((1, half, 1, n_b, FB), lambda q, z, s=s: (q, 0, z[0] ^ s, 0, 0)) for s in range(n_z)
    ]
    return pl.pallas_call(
        functools.partial(project_kernel, scale, len(hidden), n_z),
        grid_spec=pltpu.PrefetchScalarGridSpec(
            num_scalar_prefetch=1,
            grid=(n_q,),
            in_specs=[pl.BlockSpec((t, COLS), lambda q, z: (0, q))]
            + [pl.BlockSpec((rows, h.shape[1]), lambda q, z: (q, 0)) for h in hidden]
            + right_specs * 2,
            out_specs=[pl.BlockSpec((t, COLS), lambda q, z: (0, q))]
            + [pl.BlockSpec((rows, t), lambda q, z: (q, 0))] * n_z,
        ),
        out_shape=[jax.ShapeDtypeStruct((t, cols), BF)]
        + [jax.ShapeDtypeStruct((n_q * rows, t), BF)] * n_z,
        compiler_params=pltpu.CompilerParams(vmem_limit_bytes=VMEM),
        cost_estimate=cost(2 * t * cols * n_z * rows * 2, 6 * t * cols),
        name="project",
    )(z, part, *hidden, *[sides[0]] * n_z, *[sides[1]] * n_z)


def grad_right_kernel(*refs):
    *hid_refs, resid_ref, out_ref = refs
    n_z, rows = len(hid_refs), hid_refs[0].shape[1]
    hid = jnp.concatenate([r[0] for r in hid_refs], axis=0)
    prod = jnp.dot(hid, resid_ref[...], preferred_element_type=F32)
    prod = prod.reshape(n_z, GROUP, rows // GROUP, COLS)
    block = lax.broadcasted_iota(jnp.int32, (1, 1, COLS), 2) // FB
    total = prod[:, 0]
    for k in range(1, GROUP):
        total = jnp.where(block == k, prod[:, k], total)
    out_ref[...] = total.astype(BF)


def grad_right_partial(hidden, resid):
    t, cols = resid.shape
    n_z, n_q = len(hidden), cols // COLS
    rows = hidden[0][0].shape[1] // n_q
    return pl.pallas_call(
        grad_right_kernel,
        grid=(n_q,),
        in_specs=[pl.BlockSpec((1, rows, t), lambda q, i=i: (i, q, 0)) for _, i in hidden]
        + [pl.BlockSpec((t, COLS), lambda q: (0, q))],
        out_specs=pl.BlockSpec((n_z, rows // GROUP, COLS), lambda q: (0, 0, q)),
        out_shape=jax.ShapeDtypeStruct((n_z, rows // GROUP, cols), BF),
        compiler_params=pltpu.CompilerParams(vmem_limit_bytes=VMEM),
        cost_estimate=cost(2 * t * cols * n_z * rows, 2 * t * cols),
        name="grad_right",
    )(*[h for h, _ in hidden], resid)


def grad_left_kernel(n_z, n_k, *refs):
    back_refs, tok_refs, out_ref = refs[:n_z], refs[n_z:-1], refs[-1]
    total = back_refs[0][...].astype(F32)
    for ref in back_refs[1:]:
        total = total + ref[...].astype(F32)
    prod = jnp.dot(total.astype(BF), rows_of(tok_refs), preferred_element_type=F32)
    rows, block = prod.shape
    prod = prod.reshape(n_k, rows // n_k, block)
    at = pl.program_id(0) * (block // BI)
    own = lax.broadcasted_iota(jnp.int32, prod.shape, 1) == at + lax.broadcasted_iota(
        jnp.int32, prod.shape, 2
    ) // BI
    out_ref[...] = jnp.where(own, prod, 0.0).sum(1).astype(BF)


def grad_left_of(backs, tokens, n_k):
    n_z = len(backs)
    rows, t = backs[1].shape
    piece, depth = tokens[0].shape
    block = min(depth, 1024)
    return pl.pallas_call(
        functools.partial(grad_left_kernel, n_z, n_k),
        grid=(depth // block,),
        in_specs=[pl.BlockSpec((rows, t), lambda q: (0, 0))] * n_z
        + [pl.BlockSpec((piece, block), lambda q: (0, q))] * len(tokens),
        out_specs=pl.BlockSpec((n_k, block), lambda q: (0, q)),
        out_shape=jax.ShapeDtypeStruct((n_k, depth), BF),
        compiler_params=pltpu.CompilerParams(vmem_limit_bytes=VMEM),
        cost_estimate=cost(2 * t * rows * depth, 2 * t * depth),
        name="grad_left",
    )(*backs, *tokens)


def place_kernel(n_b, c_ref, *refs):
    in_refs, out_ref = refs[:-1], refs[-1]
    n_c, n_k = len(in_refs), in_refs[0].shape[0]
    x = rows_of(in_refs)
    row = lax.broadcasted_iota(jnp.int32, (NB, NB), 0)
    col = lax.broadcasted_iota(jnp.int32, (NB, NB), 1)
    pick = row == ((col // n_k) ^ c_ref[0]) * n_k + col % n_k
    got = lax.dot_general(
        x, pick.astype(F32).astype(BF), (((0,), (1,)), ((), ())), preferred_element_type=F32
    )
    for j in range(got.shape[0] // n_b):
        out_ref[:, j * NB : (j + 1) * NB] = got[j * n_b : (j + 1) * n_b]


def place(c, pieces, n_b):
    n = pieces[0].shape[1] // n_b
    return pl.pallas_call(
        functools.partial(place_kernel, n_b),
        in_specs=[pl.BlockSpec(memory_space=pltpu.SMEM)]
        + [pl.BlockSpec(memory_space=pltpu.VMEM)] * len(pieces),
        out_specs=pl.BlockSpec(memory_space=pltpu.VMEM),
        out_shape=jax.ShapeDtypeStruct((n_b, n * NB), F32),
        name="place",
    )(c, *pieces)


def swap(x, axes, s):
    n = lax.axis_size(axes)
    return lax.ppermute(x, axes, [(i, i ^ s) for i in range(n)])


def gather(x, axes):
    got = [x]
    for s in range(1, lax.axis_size(axes)):
        got.append(swap(got[s & (s - 1)], axes, s & -s))
    return got


def pick(x, at):
    return lax.dynamic_index_in_dim(x, at, 0, keepdims=False)


def per_device(tokens, teacher, left_blocks, right_blocks):
    n_z = lax.axis_size("blk")
    n_tok = lax.axis_size("tok")
    n_c = lax.axis_size(("tok", "rep"))
    z = lax.axis_index("blk")
    c = lax.axis_index(("tok", "rep"))
    plane = ("tok", "rep")
    n_b = left_blocks.shape[0]
    n_k = teacher.shape[1] // FB
    n_q = n_k // GROUP
    scale = float(tokens.shape[0] * n_c) ** (-0.5)

    left = left_blocks.reshape(n_b * BI, NB)
    rows_kb = n_k * n_b
    take = (
        lax.broadcasted_iota(jnp.int32, (rows_kb, NB), 0) // n_b + c * n_k
        == lax.broadcasted_iota(jnp.int32, (rows_kb, NB), 1)
    ).astype(BF)
    diag = (
        lax.broadcasted_iota(jnp.int32, (rows_kb, n_b * BI), 0) % n_b
        == lax.broadcasted_iota(jnp.int32, (rows_kb, n_b * BI), 1) // BI
    )
    left = lax.dot_general(take, left, NT, preferred_element_type=F32)
    left = jnp.where(diag, left, 0.0).astype(BF)

    def hidden_of(chip):
        return jnp.concatenate(
            [lax.dot_general(left, p, NT, preferred_element_type=F32).astype(BF) for p in chip], axis=1
        )

    far = [swap(tokens, "tok", s) for s in range(1, n_tok)]
    near = gather(tokens, "rep")
    first = hidden_of(near)

    sides = right_blocks.reshape(n_q, 2, GROUP // 2, n_z, n_b, FB)
    turn = [
        [(a * n_c + b, (b ^ side) * n_c + a) for a in range(n_z) for b in range(n_c)] for side in (0, n_c // 2)
    ]
    sides = [lax.ppermute(sides[:, i], ("blk",) + plane, perm) for i, perm in enumerate(turn)]
    far, first, sides = lax.optimization_barrier((far, first, sides))

    chips = [near] + [gather(x, "rep") for x in far]
    pieces = [p for chip in chips for p in chip]
    hid = [jnp.concatenate([first] + [hidden_of(chip) for chip in chips[1:]], axis=1)]
    bit = n_z // 2
    got = swap(hid[0], "blk", bit)
    part, got = lax.optimization_barrier((target(pieces, teacher), got))
    hidden, order, got = [hid[0][None]], [0], got[None]
    while True:
        hidden.append(got)
        order += [o ^ bit for o in order]
        bit //= 2
        if bit == 0:
            break
        got = swap(jnp.concatenate(hidden, axis=0), "blk", bit)
    where = [(x, i) for x in hidden for i in range(x.shape[0])]
    hidden = [where[order.index(s)] for s in range(n_z)]
    resid, *back = project(jnp.reshape(z, (1,)).astype(jnp.int32), part, hid, sides, scale)
    backs = back[:1] + [swap(back[s], "blk", s) for s in range(1, n_z)]

    gr = grad_right_partial(hidden, resid)
    there = []
    for s in range(n_c):
        piece = pick(gr, z ^ c ^ s)
        there.append(swap(piece, plane, s) if s else piece)
    there = jnp.stack(there, 0)
    total = None
    for s in range(n_z):
        piece = pick(there, c ^ z ^ s)
        piece = (swap(piece, "blk", s) if s else piece).astype(F32)
        total = piece if total is None else total + piece
    grad_right = total.reshape(n_b, n_k, FB).transpose(1, 0, 2).reshape(n_k, n_b * FB)

    gl = grad_left_of(backs, pieces, n_k)
    gl = gl.reshape(n_k, n_b, n_c, BI // n_c).transpose(2, 0, 3, 1).reshape(n_c, n_k, -1)
    got = []
    for s in range(n_c):
        piece = pick(gl, c ^ s)
        got.append(swap(piece, plane, s) if s else piece)
    grad_left = place(jnp.reshape(c, (1,)).astype(jnp.int32), got, n_b)

    return grad_left, grad_right


def solution(mesh):
    return jax.shard_map(
        per_device,
        mesh=mesh,
        in_specs=(
            P(("layer", "tok", "rep"), "blk"),
            P(("layer", "blk"), ("tok", "rep")),
            P(("layer", "blk"), None),
            P(("layer", "blk"), None),
        ),
        out_specs=(P(("layer", "blk"), ("tok", "rep")), P(("layer", "blk"), ("tok", "rep"))),
        check_vma=False,
    )
```

```python
import functools

import jax
import jax.numpy as jnp
from jax import lax
from jax.experimental import pallas as pl
from jax.experimental.pallas import tpu as pltpu
from jax.sharding import PartitionSpec as P

D = 8192
F = 14336
NB = 64
BI = D // NB
FB = F // NB
GROUP = 4
COLS = GROUP * FB
BF = jnp.bfloat16
F32 = jnp.float32
NT = (((1,), (1,)), ((), ()))
TN = (((0,), (0,)), ((), ()))
SPLIT = 4
VMEM = 40 * 1024 * 1024


def cost(flops, nbytes):
    return pl.CostEstimate(flops=flops, bytes_accessed=nbytes, transcendentals=0)


def rows_of(refs):
    return jnp.concatenate([r[...] for r in refs], axis=0) if len(refs) > 1 else refs[0][...]


def spread(right):
    n_z, n_k, n_b, _ = right.shape
    rows = n_z * n_k * n_b
    col = lax.broadcasted_iota(jnp.int32, (1, COLS), 1)
    tile = (lax.broadcasted_iota(jnp.int32, (FB, 1), 0) == col % FB).astype(F32).astype(BF)
    wide = jnp.dot(right.reshape(rows, FB), tile, preferred_element_type=F32)
    k_row = lax.broadcasted_iota(jnp.int32, (rows, 1), 0) // n_b % n_k
    return jnp.where(k_row == col // FB, wide, 0.0).astype(BF)


def target_kernel(pieces, *refs):
    tok_refs, teacher_refs, out_ref = refs[:pieces], refs[pieces:-1], refs[-1]
    out_ref[...] = jnp.dot(rows_of(tok_refs), rows_of(teacher_refs), preferred_element_type=F32).astype(BF)


def target(tokens, teacher):
    t, depth = tokens[0].shape
    cols = teacher.shape[1]
    block = 512 if cols % 512 == 0 else COLS
    total = t * len(tokens)
    return pl.pallas_call(
        functools.partial(target_kernel, len(tokens)),
        grid=(cols // block,),
        in_specs=[pl.BlockSpec((t, depth), lambda q: (0, 0))] * len(tokens)
        + [pl.BlockSpec((depth // SPLIT, block), lambda q, i=i: (i, q)) for i in range(SPLIT)],
        out_specs=pl.BlockSpec((total, block), lambda q: (0, q)),
        out_shape=jax.ShapeDtypeStruct((total, cols), BF),
        compiler_params=pltpu.CompilerParams(vmem_limit_bytes=VMEM),
        cost_estimate=cost(2 * total * cols * depth, 2 * depth * cols),
        name="target",
    )(*tokens, *[teacher] * SPLIT)


def project_kernel(scale, n_hid, n_z, z_ref, part_ref, *refs):
    hid_refs, right_refs, (resid_ref, back_ref) = refs[:n_hid], refs[n_hid:-2], refs[-2:]
    right = jnp.stack(
        [jnp.concatenate([a[0, :, 0], b[0, :, 0]], axis=0) for a, b in zip(right_refs[:n_z], right_refs[n_z:])],
        axis=0,
    )
    right = spread(right)
    rows = right.shape[0] // n_z
    hid = jnp.concatenate([h[...] for h in hid_refs], axis=1)
    student = lax.dot_general(hid, right[:rows], TN, preferred_element_type=F32)
    resid = ((student - part_ref[...].astype(F32)) * scale).astype(BF)
    resid_ref[...] = resid
    back = lax.dot_general(right, resid, NT, preferred_element_type=F32)
    back_ref[...] = back.astype(BF).reshape(back_ref.shape)


def project(z, part, hidden, sides, scale):
    t, cols = part.shape
    n_q, half, n_z, n_b, _ = sides[0].shape
    rows = GROUP * n_b
    right_specs = [
        pl.BlockSpec((1, half, 1, n_b, FB), lambda q, z, s=s: (q, 0, z[0] ^ s, 0, 0)) for s in range(n_z)
    ]
    return pl.pallas_call(
        functools.partial(project_kernel, scale, len(hidden), n_z),
        grid_spec=pltpu.PrefetchScalarGridSpec(
            num_scalar_prefetch=1,
            grid=(n_q,),
            in_specs=[pl.BlockSpec((t, COLS), lambda q, z: (0, q))]
            + [pl.BlockSpec((rows, h.shape[1]), lambda q, z: (q, 0)) for h in hidden]
            + right_specs * 2,
            out_specs=[
                pl.BlockSpec((t, COLS), lambda q, z: (0, q)),
                pl.BlockSpec((n_z, rows, t), lambda q, z: (0, q, 0)),
            ],
        ),
        out_shape=[
            jax.ShapeDtypeStruct((t, cols), BF),
            jax.ShapeDtypeStruct((n_z, n_q * rows, t), BF),
        ],
        compiler_params=pltpu.CompilerParams(vmem_limit_bytes=VMEM),
        cost_estimate=cost(2 * t * cols * n_z * rows * 2, 6 * t * cols),
        name="project",
    )(z, part, *hidden, *[sides[0]] * n_z, *[sides[1]] * n_z)


def grad_right_kernel(n_z, parts, *refs):
    hid_refs, (resid_ref, out_ref) = refs[:-2], refs[-2:]
    hid = jnp.concatenate(
        [
            jnp.concatenate([r[...] for r in hid_refs[s * parts : (s + 1) * parts]], axis=1)
            for s in range(n_z)
        ],
        axis=0,
    )
    prod = jnp.dot(hid, resid_ref[...], preferred_element_type=F32)
    prod = prod.reshape(n_z, GROUP, prod.shape[0] // (n_z * GROUP), COLS)
    block = lax.broadcasted_iota(jnp.int32, (1, 1, COLS), 2) // FB
    total = prod[:, 0]
    for k in range(1, GROUP):
        total = jnp.where(block == k, prod[:, k], total)
    out_ref[...] = total.astype(BF)


def grad_right_partial(hidden, resid):
    t, cols = resid.shape
    n_z, parts = len(hidden), len(hidden[0])
    n_q = cols // COLS
    rows = hidden[0][0].shape[0] // n_q
    return pl.pallas_call(
        functools.partial(grad_right_kernel, n_z, parts),
        grid=(n_q,),
        in_specs=[pl.BlockSpec((rows, h.shape[1]), lambda q: (q, 0)) for hs in hidden for h in hs]
        + [pl.BlockSpec((t, COLS), lambda q: (0, q))],
        out_specs=pl.BlockSpec((n_z, rows // GROUP, COLS), lambda q: (0, 0, q)),
        out_shape=jax.ShapeDtypeStruct((n_z, rows // GROUP, cols), BF),
        compiler_params=pltpu.CompilerParams(vmem_limit_bytes=VMEM),
        cost_estimate=cost(2 * t * cols * n_z * rows, 2 * t * cols),
        name="grad_right",
    )(*[h for hs in hidden for h in hs], resid)


def grad_left_kernel(n_z, n_k, *refs):
    back_refs, tok_refs, out_ref = refs[:n_z], refs[n_z:-1], refs[-1]
    total = back_refs[0][0].astype(F32)
    for ref in back_refs[1:]:
        total = total + ref[...].astype(F32)
    prod = jnp.dot(total.astype(BF), rows_of(tok_refs), preferred_element_type=F32)
    rows, block = prod.shape
    prod = prod.reshape(n_k, rows // n_k, block)
    at = pl.program_id(0) * (block // BI)
    own = lax.broadcasted_iota(jnp.int32, prod.shape, 1) == at + lax.broadcasted_iota(
        jnp.int32, prod.shape, 2
    ) // BI
    out_ref[...] = jnp.where(own, prod, 0.0).sum(1).astype(BF)


def grad_left_of(backs, tokens, n_k):
    n_z = len(backs)
    rows, t = backs[1].shape
    piece, depth = tokens[0].shape
    block = min(depth, 1024)
    return pl.pallas_call(
        functools.partial(grad_left_kernel, n_z, n_k),
        grid=(depth // block,),
        in_specs=[pl.BlockSpec((1, rows, t), lambda q: (0, 0, 0))]
        + [pl.BlockSpec((rows, t), lambda q: (0, 0))] * (n_z - 1)
        + [pl.BlockSpec((piece, block), lambda q: (0, q))] * len(tokens),
        out_specs=pl.BlockSpec((n_k, block), lambda q: (0, q)),
        out_shape=jax.ShapeDtypeStruct((n_k, depth), BF),
        compiler_params=pltpu.CompilerParams(vmem_limit_bytes=VMEM),
        cost_estimate=cost(2 * t * rows * depth, 2 * t * depth),
        name="grad_left",
    )(*backs, *tokens)


def place_kernel(n_b, c_ref, *refs):
    in_refs, out_ref = refs[:-1], refs[-1]
    n_c, n_k = len(in_refs), in_refs[0].shape[0]
    x = rows_of(in_refs)
    row = lax.broadcasted_iota(jnp.int32, (NB, NB), 0)
    col = lax.broadcasted_iota(jnp.int32, (NB, NB), 1)
    pick = row == ((col // n_k) ^ c_ref[0]) * n_k + col % n_k
    got = lax.dot_general(
        x, pick.astype(F32).astype(BF), (((0,), (1,)), ((), ())), preferred_element_type=F32
    )
    for j in range(got.shape[0] // n_b):
        out_ref[:, j * NB : (j + 1) * NB] = got[j * n_b : (j + 1) * n_b]


def place(c, pieces, n_b):
    n = pieces[0].shape[1] // n_b
    return pl.pallas_call(
        functools.partial(place_kernel, n_b),
        in_specs=[pl.BlockSpec(memory_space=pltpu.SMEM)]
        + [pl.BlockSpec(memory_space=pltpu.VMEM)] * len(pieces),
        out_specs=pl.BlockSpec(memory_space=pltpu.VMEM),
        out_shape=jax.ShapeDtypeStruct((n_b, n * NB), F32),
        name="place",
    )(c, *pieces)


def swap(x, axes, s):
    n = lax.axis_size(axes)
    return lax.ppermute(x, axes, [(i, i ^ s) for i in range(n)])


def gather(x, axes):
    got = [x]
    for s in range(1, lax.axis_size(axes)):
        got.append(swap(got[s & (s - 1)], axes, s & -s))
    return got


def pick(x, at):
    return lax.dynamic_index_in_dim(x, at, 0, keepdims=False)


def per_device(tokens, teacher, left_blocks, right_blocks):
    n_z = lax.axis_size("blk")
    n_tok = lax.axis_size("tok")
    n_c = lax.axis_size(("tok", "rep"))
    z = lax.axis_index("blk")
    c = lax.axis_index(("tok", "rep"))
    plane = ("tok", "rep")
    n_b = left_blocks.shape[0]
    n_k = teacher.shape[1] // FB
    n_q = n_k // GROUP
    scale = float(tokens.shape[0] * n_c) ** (-0.5)

    left = left_blocks.reshape(n_b * BI, NB)
    rows_kb = n_k * n_b
    take = (
        lax.broadcasted_iota(jnp.int32, (rows_kb, NB), 0) // n_b + c * n_k
        == lax.broadcasted_iota(jnp.int32, (rows_kb, NB), 1)
    ).astype(BF)
    diag = (
        lax.broadcasted_iota(jnp.int32, (rows_kb, n_b * BI), 0) % n_b
        == lax.broadcasted_iota(jnp.int32, (rows_kb, n_b * BI), 1) // BI
    )
    left = lax.dot_general(take, left, NT, preferred_element_type=F32)
    left = jnp.where(diag, left, 0.0).astype(BF)

    def hidden_of(chip):
        return jnp.concatenate(
            [lax.dot_general(left, p, NT, preferred_element_type=F32).astype(BF) for p in chip], axis=1
        )

    far = [swap(tokens, "tok", s) for s in range(1, n_tok)]
    near = gather(tokens, "rep")
    first = hidden_of(near)

    sides = right_blocks.reshape(n_q, 2, GROUP // 2, n_z, n_b, FB)
    turn = [
        [(a * n_c + b, (b ^ side) * n_c + a) for a in range(n_z) for b in range(n_c)] for side in (0, n_c // 2)
    ]
    sides = [lax.ppermute(sides[:, i], ("blk",) + plane, perm) for i, perm in enumerate(turn)]
    far, first, sides = lax.optimization_barrier((far, first, sides))

    chips = [near] + [gather(x, "rep") for x in far]
    pieces = [p for chip in chips for p in chip]
    hid = [jnp.concatenate([first] + [hidden_of(chip) for chip in chips[1:]], axis=1)]
    two = swap(hid[0], "blk", 2)
    hidden = hid + [swap(hid[0], "blk", 1), two]
    part, hidden[1:] = lax.optimization_barrier((target(pieces, teacher), hidden[1:]))
    for s in range(3, n_z):
        hidden.append(swap(hidden[s & (s - 1)], "blk", s & -s))
    hidden = [[h] for h in hidden]
    resid, back = project(jnp.reshape(z, (1,)).astype(jnp.int32), part, hid, sides, scale)
    far_first = list(range(2, n_z)) + [1]
    backs = [back] + [swap(back[s], "blk", s) for s in far_first]

    gr = grad_right_partial(hidden, resid)
    there = []
    for s in range(n_c):
        piece = pick(gr, z ^ c ^ s)
        there.append(swap(piece, plane, s) if s else piece)
    there = jnp.stack(there, 0)
    total = pick(there, c ^ z).astype(F32)
    for s in far_first:
        total = total + swap(pick(there, c ^ z ^ s), "blk", s).astype(F32)
    grad_right = total.reshape(n_b, n_k, FB).transpose(1, 0, 2).reshape(n_k, n_b * FB)

    gl = grad_left_of(backs, pieces, n_k)
    gl = gl.reshape(n_k, n_b, n_c, BI // n_c).transpose(2, 0, 3, 1).reshape(n_c, n_k, -1)
    got = []
    for s in range(n_c):
        piece = pick(gl, c ^ s)
        got.append(swap(piece, plane, s) if s else piece)
    grad_left = place(jnp.reshape(c, (1,)).astype(jnp.int32), got, n_b)

    return grad_left, grad_right


def solution(mesh):
    return jax.shard_map(
        per_device,
        mesh=mesh,
        in_specs=(
            P(("layer", "tok", "rep"), "blk"),
            P(("layer", "blk"), ("tok", "rep")),
            P(("layer", "blk"), None),
            P(("layer", "blk"), None),
        ),
        out_specs=(P(("layer", "blk"), ("tok", "rep")), P(("layer", "blk"), ("tok", "rep"))),
        check_vma=False,
    )
```

```python
import functools

import jax
import jax.numpy as jnp
from jax import lax
from jax.experimental import pallas as pl
from jax.experimental.pallas import tpu as pltpu
from jax.sharding import PartitionSpec as P

D = 8192
F = 14336
NB = 64
BI = D // NB
FB = F // NB
GROUP = 4
COLS = GROUP * FB
BF = jnp.bfloat16
F32 = jnp.float32
NT = (((1,), (1,)), ((), ()))
TN = (((0,), (0,)), ((), ()))
SPLIT = 4
VMEM = 40 * 1024 * 1024


def cost(flops, nbytes):
    return pl.CostEstimate(flops=flops, bytes_accessed=nbytes, transcendentals=0)


def rows_of(refs):
    return jnp.concatenate([r[...] for r in refs], axis=0) if len(refs) > 1 else refs[0][...]


def spread(right):
    n_z, n_k, n_b, _ = right.shape
    rows = n_z * n_k * n_b
    col = lax.broadcasted_iota(jnp.int32, (1, COLS), 1)
    tile = (lax.broadcasted_iota(jnp.int32, (FB, 1), 0) == col % FB).astype(F32).astype(BF)
    wide = jnp.dot(right.reshape(rows, FB), tile, preferred_element_type=F32)
    k_row = lax.broadcasted_iota(jnp.int32, (rows, 1), 0) // n_b % n_k
    return jnp.where(k_row == col // FB, wide, 0.0).astype(BF)


def target_kernel(pieces, *refs):
    tok_refs, teacher_refs, out_ref = refs[:pieces], refs[pieces:-1], refs[-1]
    out_ref[...] = jnp.dot(rows_of(tok_refs), rows_of(teacher_refs), preferred_element_type=F32).astype(BF)


def target(tokens, teacher):
    t, depth = tokens[0].shape
    cols = teacher.shape[1]
    block = 512 if cols % 512 == 0 else COLS
    total = t * len(tokens)
    return pl.pallas_call(
        functools.partial(target_kernel, len(tokens)),
        grid=(cols // block,),
        in_specs=[pl.BlockSpec((t, depth), lambda q: (0, 0))] * len(tokens)
        + [pl.BlockSpec((depth // SPLIT, block), lambda q, i=i: (i, q)) for i in range(SPLIT)],
        out_specs=pl.BlockSpec((total, block), lambda q: (0, q)),
        out_shape=jax.ShapeDtypeStruct((total, cols), BF),
        compiler_params=pltpu.CompilerParams(vmem_limit_bytes=VMEM),
        cost_estimate=cost(2 * total * cols * depth, 2 * depth * cols),
        name="target",
    )(*tokens, *[teacher] * SPLIT)


def project_kernel(scale, n_hid, n_z, z_ref, part_ref, *refs):
    hid_refs, right_refs, (resid_ref, back_ref) = refs[:n_hid], refs[n_hid:-2], refs[-2:]
    right = jnp.stack(
        [jnp.concatenate([a[0, :, 0], b[0, :, 0]], axis=0) for a, b in zip(right_refs[:n_z], right_refs[n_z:])],
        axis=0,
    )
    right = spread(right)
    rows = right.shape[0] // n_z
    hid = jnp.concatenate([h[...] for h in hid_refs], axis=1)
    student = lax.dot_general(hid, right[:rows], TN, preferred_element_type=F32)
    resid = ((student - part_ref[...].astype(F32)) * scale).astype(BF)
    resid_ref[...] = resid
    back = lax.dot_general(right, resid, NT, preferred_element_type=F32)
    back_ref[...] = back.astype(BF).reshape(back_ref.shape)


def project(z, part, hidden, sides, scale):
    t, cols = part.shape
    n_q, half, n_z, n_b, _ = sides[0].shape
    rows = GROUP * n_b
    right_specs = [
        pl.BlockSpec((1, half, 1, n_b, FB), lambda q, z, s=s: (q, 0, z[0] ^ s, 0, 0)) for s in range(n_z)
    ]
    return pl.pallas_call(
        functools.partial(project_kernel, scale, len(hidden), n_z),
        grid_spec=pltpu.PrefetchScalarGridSpec(
            num_scalar_prefetch=1,
            grid=(n_q,),
            in_specs=[pl.BlockSpec((t, COLS), lambda q, z: (0, q))]
            + [pl.BlockSpec((rows, h.shape[1]), lambda q, z: (q, 0)) for h in hidden]
            + right_specs * 2,
            out_specs=[
                pl.BlockSpec((t, COLS), lambda q, z: (0, q)),
                pl.BlockSpec((n_z, rows, t), lambda q, z: (0, q, 0)),
            ],
        ),
        out_shape=[
            jax.ShapeDtypeStruct((t, cols), BF),
            jax.ShapeDtypeStruct((n_z, n_q * rows, t), BF),
        ],
        compiler_params=pltpu.CompilerParams(vmem_limit_bytes=VMEM),
        cost_estimate=cost(2 * t * cols * n_z * rows * 2, 6 * t * cols),
        name="project",
    )(z, part, *hidden, *[sides[0]] * n_z, *[sides[1]] * n_z)


def grad_right_kernel(n_z, parts, *refs):
    hid_refs, (resid_ref, out_ref) = refs[:-2], refs[-2:]
    hid = jnp.concatenate(
        [
            jnp.concatenate([r[...] for r in hid_refs[s * parts : (s + 1) * parts]], axis=1)
            for s in range(n_z)
        ],
        axis=0,
    )
    prod = jnp.dot(hid, resid_ref[...], preferred_element_type=F32)
    prod = prod.reshape(n_z, GROUP, prod.shape[0] // (n_z * GROUP), COLS)
    block = lax.broadcasted_iota(jnp.int32, (1, 1, COLS), 2) // FB
    total = prod[:, 0]
    for k in range(1, GROUP):
        total = jnp.where(block == k, prod[:, k], total)
    out_ref[...] = total.astype(BF)


def grad_right_partial(hidden, resid):
    t, cols = resid.shape
    n_z, parts = len(hidden), len(hidden[0])
    n_q = cols // COLS
    rows = hidden[0][0].shape[0] // n_q
    return pl.pallas_call(
        functools.partial(grad_right_kernel, n_z, parts),
        grid=(n_q,),
        in_specs=[pl.BlockSpec((rows, h.shape[1]), lambda q: (q, 0)) for hs in hidden for h in hs]
        + [pl.BlockSpec((t, COLS), lambda q: (0, q))],
        out_specs=pl.BlockSpec((n_z, rows // GROUP, COLS), lambda q: (0, 0, q)),
        out_shape=jax.ShapeDtypeStruct((n_z, rows // GROUP, cols), BF),
        compiler_params=pltpu.CompilerParams(vmem_limit_bytes=VMEM),
        cost_estimate=cost(2 * t * cols * n_z * rows, 2 * t * cols),
        name="grad_right",
    )(*[h for hs in hidden for h in hs], resid)


def grad_left_kernel(n_z, n_k, *refs):
    back_refs, tok_refs, out_ref = refs[:n_z], refs[n_z:-1], refs[-1]
    total = back_refs[0][0].astype(F32)
    for ref in back_refs[1:]:
        total = total + ref[...].astype(F32)
    prod = jnp.dot(total.astype(BF), rows_of(tok_refs), preferred_element_type=F32)
    rows, block = prod.shape
    prod = prod.reshape(n_k, rows // n_k, block)
    at = pl.program_id(0) * (block // BI)
    own = lax.broadcasted_iota(jnp.int32, prod.shape, 1) == at + lax.broadcasted_iota(
        jnp.int32, prod.shape, 2
    ) // BI
    out_ref[...] = jnp.where(own, prod, 0.0).sum(1).astype(BF)


def grad_left_of(backs, tokens, n_k):
    n_z = len(backs)
    rows, t = backs[1].shape
    piece, depth = tokens[0].shape
    block = min(depth, 1024)
    return pl.pallas_call(
        functools.partial(grad_left_kernel, n_z, n_k),
        grid=(depth // block,),
        in_specs=[pl.BlockSpec((1, rows, t), lambda q: (0, 0, 0))]
        + [pl.BlockSpec((rows, t), lambda q: (0, 0))] * (n_z - 1)
        + [pl.BlockSpec((piece, block), lambda q: (0, q))] * len(tokens),
        out_specs=pl.BlockSpec((n_k, block), lambda q: (0, q)),
        out_shape=jax.ShapeDtypeStruct((n_k, depth), BF),
        compiler_params=pltpu.CompilerParams(vmem_limit_bytes=VMEM),
        cost_estimate=cost(2 * t * rows * depth, 2 * t * depth),
        name="grad_left",
    )(*backs, *tokens)


def place_kernel(n_b, c_ref, *refs):
    in_refs, out_ref = refs[:-1], refs[-1]
    n_c, n_k = len(in_refs), in_refs[0].shape[0]
    x = rows_of(in_refs)
    row = lax.broadcasted_iota(jnp.int32, (NB, NB), 0)
    col = lax.broadcasted_iota(jnp.int32, (NB, NB), 1)
    pick = row == ((col // n_k) ^ c_ref[0]) * n_k + col % n_k
    got = lax.dot_general(
        x, pick.astype(F32).astype(BF), (((0,), (1,)), ((), ())), preferred_element_type=F32
    )
    for j in range(got.shape[0] // n_b):
        out_ref[:, j * NB : (j + 1) * NB] = got[j * n_b : (j + 1) * n_b]


def place(c, pieces, n_b):
    n = pieces[0].shape[1] // n_b
    return pl.pallas_call(
        functools.partial(place_kernel, n_b),
        in_specs=[pl.BlockSpec(memory_space=pltpu.SMEM)]
        + [pl.BlockSpec(memory_space=pltpu.VMEM)] * len(pieces),
        out_specs=pl.BlockSpec(memory_space=pltpu.VMEM),
        out_shape=jax.ShapeDtypeStruct((n_b, n * NB), F32),
        name="place",
    )(c, *pieces)


def swap(x, axes, s):
    n = lax.axis_size(axes)
    return lax.ppermute(x, axes, [(i, i ^ s) for i in range(n)])


def gather(x, axes):
    got = [x]
    for s in range(1, lax.axis_size(axes)):
        got.append(swap(got[s & (s - 1)], axes, s & -s))
    return got


def pick(x, at):
    return lax.dynamic_index_in_dim(x, at, 0, keepdims=False)


def per_device(tokens, teacher, left_blocks, right_blocks):
    n_z = lax.axis_size("blk")
    n_tok = lax.axis_size("tok")
    n_c = lax.axis_size(("tok", "rep"))
    z = lax.axis_index("blk")
    c = lax.axis_index(("tok", "rep"))
    plane = ("tok", "rep")
    n_b = left_blocks.shape[0]
    n_k = teacher.shape[1] // FB
    n_q = n_k // GROUP
    scale = float(tokens.shape[0] * n_c) ** (-0.5)

    left = left_blocks.reshape(n_b * BI, NB)
    rows_kb = n_k * n_b
    take = (
        lax.broadcasted_iota(jnp.int32, (rows_kb, NB), 0) // n_b + c * n_k
        == lax.broadcasted_iota(jnp.int32, (rows_kb, NB), 1)
    ).astype(BF)
    diag = (
        lax.broadcasted_iota(jnp.int32, (rows_kb, n_b * BI), 0) % n_b
        == lax.broadcasted_iota(jnp.int32, (rows_kb, n_b * BI), 1) // BI
    )
    left = lax.dot_general(take, left, NT, preferred_element_type=F32)
    left = jnp.where(diag, left, 0.0).astype(BF)

    def hidden_of(chip):
        return jnp.concatenate(
            [lax.dot_general(left, p, NT, preferred_element_type=F32).astype(BF) for p in chip], axis=1
        )

    far = [swap(tokens, "tok", s) for s in range(1, n_tok)]
    near = gather(tokens, "rep")
    first = hidden_of(near)

    sides = right_blocks.reshape(n_q, 2, GROUP // 2, n_z, n_b, FB)
    turn = [
        [(a * n_c + b, (b ^ side) * n_c + a) for a in range(n_z) for b in range(n_c)] for side in (0, n_c // 2)
    ]
    sides = [lax.ppermute(sides[:, i], ("blk",) + plane, perm) for i, perm in enumerate(turn)]
    far, first, sides = lax.optimization_barrier((far, first, sides))

    chips = [near] + [gather(x, "rep") for x in far]
    pieces = [p for chip in chips for p in chip]
    hid = [jnp.concatenate([first] + [hidden_of(chip) for chip in chips[1:]], axis=1)]
    two, one = swap(hid[0], "blk", 2), swap(hid[0], "blk", 1)
    part, two, one = lax.optimization_barrier((target(pieces, teacher), two, one))
    hidden = hid + [one, two]
    for s in range(3, n_z):
        hidden.append(swap(hidden[s & (s - 1)], "blk", s & -s))
    hidden = [[h] for h in hidden]
    resid, back = project(jnp.reshape(z, (1,)).astype(jnp.int32), part, hid, sides, scale)
    far_first = list(range(2, n_z)) + [1]
    backs = [back] + [swap(back[s], "blk", s) for s in far_first]

    gr = grad_right_partial(hidden, resid)
    there = []
    for s in range(n_c):
        piece = pick(gr, z ^ c ^ s)
        there.append(swap(piece, plane, s) if s else piece)
    there = jnp.stack(there, 0)
    total = pick(there, c ^ z).astype(F32)
    for s in far_first:
        total = total + swap(pick(there, c ^ z ^ s), "blk", s).astype(F32)
    grad_right = total.reshape(n_b, n_k, FB).transpose(1, 0, 2).reshape(n_k, n_b * FB)

    gl = grad_left_of(backs, pieces, n_k)
    gl = gl.reshape(n_k, n_b, n_c, BI // n_c).transpose(2, 0, 3, 1).reshape(n_c, n_k, -1)
    got = []
    for s in range(n_c):
        piece = pick(gl, c ^ s)
        got.append(swap(piece, plane, s) if s else piece)
    grad_left = place(jnp.reshape(c, (1,)).astype(jnp.int32), got, n_b)

    return grad_left, grad_right


def solution(mesh):
    return jax.shard_map(
        per_device,
        mesh=mesh,
        in_specs=(
            P(("layer", "tok", "rep"), "blk"),
            P(("layer", "blk"), ("tok", "rep")),
            P(("layer", "blk"), None),
            P(("layer", "blk"), None),
        ),
        out_specs=(P(("layer", "blk"), ("tok", "rep")), P(("layer", "blk"), ("tok", "rep"))),
        check_vma=False,
    )
```
